128 devices in a mesh: section: 2 (over z_hi), dp: 4 (over z_lo, core), seq: 16 (over x, y).
Axes of the slice: x: 4, y: 4, z: 4 (z_hi: 2, z_lo: 2; z = z_hi * 2 + z_lo), core: 2. Of those that a mesh axis runs over, the one named last changes fastest.
Arguments:
- enc_states: bfloat16 [8, 2048, 4096], P(('section', 'dp'), 'seq'), may hold values from -6 to 6
- enc_gain: float32 [4096], replicated, may hold values from 0.1 to 1.9
- key_weight: bfloat16 [4096, 4096], P(None, 'seq'), may hold values from -0.09375 to 0.09375
- value_weight: bfloat16 [4096, 4096], P(None, 'seq'), may hold values from -0.09375 to 0.09375
- queries: bfloat16 [8, 512, 4096], P(('section', 'dp'), None, 'seq'), may hold values from -28 to 28
- out_grad: bfloat16 [8, 512, 4096], P(('section', 'dp'), None, 'seq'), may hold values from -6 to 6
- lengths: int32 [8], replicated, may hold values from 1024 to 2048, as said below
Outputs:
- attended: bfloat16 [8, 512, 4096], P(('section', 'dp'), None, 'seq')
- enc_grad: bfloat16 [8, 2048, 4096], P(('section', 'dp'), 'seq')
- key_grad: float32 [4096, 4096], P(('section', 'dp'), 'seq')
- value_grad: float32 [4096, 4096], P(('section', 'dp'), 'seq')
- query_grad: bfloat16 [8, 512, 4096], P(('section', 'dp'), None, 'seq')
The draws below stay inside these ranges and needn't reach their ends.
Inputs may be any that keep to these rules, and one draw needn't show every extreme that they name: `lengths`: positions at or beyond a sequence's length are padding; at least one sequence in every draw has length 2048.
All inputs are finite; a program needn't handle non-finite values.
Results may differ from the reference program's by a relative error of at most 0.023.
The reference program's roundings to bfloat16 on the way (of `normed`, `prob_weights`, `grad_scores` and `row_grad`) count: a program that leaves them out, or rounds other values in their place, can miss the bound.
Values may be sent and summed in bfloat16 or wider, within the bound.
A program may use at most 128 MiB of HBM per device.

```python
import jax
import jax.numpy as jnp
from jax import lax

D = 4096
HEADS = 16
HD = 256
TGT = 512
SRC = 2048
HEADS_DEV = 1
BATCH = 8


def draw_queries(key, part):
    key = jax.random.fold_in(key, 7)
    first = jax.random.fold_in(key, 0)
    shape = (BATCH, TGT, HEADS * HD)
    base = jnp.clip(jax.random.normal(first, shape, jnp.float32), -6.0, 6.0)
    return base.astype(jnp.bfloat16)


def draw_lengths(key, part):
    key = jax.random.fold_in(key, 5)
    first, second = jax.random.split(key)
    drawn = jax.random.randint(first, (BATCH,), SRC // 2, SRC + 1)
    chosen = jax.random.randint(second, (), 0, BATCH)
    return jnp.where(jnp.arange(BATCH) == chosen, SRC, drawn).astype(jnp.int32)


def block_scale(stream_key, dims, cuts, smallest, high):
    def one(dim, shards_of):
        steps = jax.random.uniform(jax.random.fold_in(jax.random.fold_in(stream_key, 6), dim), (shards_of,), jnp.float32, smallest / len(cuts), high / len(cuts))
        return jnp.repeat(jnp.exp(steps), dims[dim] // shards_of).reshape((-1,) + (1,) * (len(dims) - dim - 1))

    level = one(*cuts[0])
    for cut in cuts[1:]:
        level = level * one(*cut)
    return level


def centred(key, extent, deviation, bound, cuts=(), kind=jnp.bfloat16):
    factor_of = block_scale(key, extent, cuts, -0.22, 0.18) if cuts else 1.0
    entries = jax.random.normal(key, extent, jnp.float32) * deviation * factor_of
    return jnp.minimum(jnp.maximum(entries, -bound), bound).astype(kind)


def setup_inputs(seed: int = 0) -> dict:
    key_of = jax.random.split(jax.random.key(seed), 8)
    return {
        "enc_states": centred(key_of[0], (BATCH, SRC, D), 1.0, 6.0, ((0, 8), (1, 16))),
        "enc_gain": jnp.clip(1.0 + 0.18 * jax.random.normal(key_of[1], (D,), jnp.float32), 0.1, 1.9),
        "key_weight": centred(key_of[2], (D, HEADS * HD), D ** -0.5, 0.09375, ((1, 16),)),
        "value_weight": centred(key_of[3], (D, HEADS * HD), D ** -0.5, 0.09375, ((1, 16),)),
        "queries": draw_queries(jax.random.fold_in(key_of[7], 71), 0),
        "out_grad": centred(key_of[5], (BATCH, TGT, HEADS * HD), 1.0, 6.0, ((0, 8), (2, 16))),
        "lengths": draw_lengths(jax.random.fold_in(key_of[7], 71), 0),
    }


EPS = 1e-06
NEG_FILL = -1e+30

def normalize(enc_rows, gain):
    wide_rows = enc_rows.astype(jnp.float32)
    factor = lax.rsqrt(lax.optimization_barrier(jnp.mean(wide_rows * wide_rows, axis=-1, keepdims=True)) + EPS)
    return ((wide_rows * factor * gain).astype(jnp.bfloat16), factor)

def norm_backward(enc_rows, factor, gain, row_grad):
    wide_rows = enc_rows.astype(jnp.float32)
    scaled = row_grad.astype(jnp.float32) * gain
    inner_sum = lax.optimization_barrier(jnp.mean(scaled * wide_rows, axis=-1, keepdims=True))
    return (factor * scaled - wide_rows * factor * factor * factor * inner_sum).astype(jnp.bfloat16)

def attend(query_rows, key_rows, value_rows, upstream, visible):
    score_scale = HD ** (-0.5)
    query_wide = query_rows.astype(jnp.float32)
    key_wide = key_rows.astype(jnp.float32)
    value_wide = value_rows.astype(jnp.float32)
    upstream_wide = upstream.astype(jnp.float32)
    scores = jnp.einsum('thd,shd->hts', query_wide, key_wide) * score_scale
    scores = jnp.where(visible[None, None, :], scores, NEG_FILL)
    row_max = lax.optimization_barrier(jnp.max(scores, axis=-1, keepdims=True))
    exponent = jnp.exp(scores - row_max)
    probability = exponent / lax.optimization_barrier(jnp.sum(exponent, axis=-1, keepdims=True))
    prob_weights = probability.astype(jnp.bfloat16).astype(jnp.float32)
    attended = jnp.einsum('hts,shd->thd', prob_weights, value_wide).astype(jnp.bfloat16)
    grad_probs = jnp.einsum('thd,shd->hts', upstream_wide, value_wide)
    inner_sum = lax.optimization_barrier(jnp.sum(probability * grad_probs, axis=-1, keepdims=True))
    grad_scores = (probability * (grad_probs - inner_sum) * score_scale).astype(jnp.bfloat16).astype(jnp.float32)
    query_grad = jnp.einsum('hts,shd->thd', grad_scores, key_wide).astype(jnp.bfloat16)
    key_grad = jnp.einsum('hts,thd->shd', grad_scores, query_wide).astype(jnp.bfloat16)
    value_grad = jnp.einsum('hts,thd->shd', prob_weights, upstream_wide).astype(jnp.bfloat16)
    return (attended, query_grad, key_grad, value_grad)

def split_heads(block, count, group_count):
    return block.reshape(count, group_count, HEADS_DEV, HD).transpose(1, 0, 2, 3)

def merge_heads(block, count):
    return block.transpose(1, 0, 2, 3).reshape(count, HEADS * HD)

def reference(enc_states, enc_gain, key_weight, value_weight, queries, out_grad, lengths):
    group_count = HEADS // HEADS_DEV
    group_width = HEADS_DEV * HD
    positions = jnp.arange(SRC, dtype=jnp.int32)
    key_blocks = key_weight.reshape(D, group_count, group_width).transpose(1, 0, 2)
    value_blocks = value_weight.reshape(D, group_count, group_width).transpose(1, 0, 2)
    key_total = jnp.zeros((D, HEADS * HD), jnp.float32)
    value_total = jnp.zeros((D, HEADS * HD), jnp.float32)
    attended_list = []
    query_list = []
    grad_list = [None] * BATCH
    for target in range(BATCH):
        partner = (target + BATCH // 2) % BATCH
        normed, factor = normalize(enc_states[partner], enc_gain)
        key_rows = jnp.dot(normed, key_weight, preferred_element_type=jnp.float32).astype(jnp.bfloat16)
        value_rows = jnp.dot(normed, value_weight, preferred_element_type=jnp.float32).astype(jnp.bfloat16)
        visible = positions < lengths[partner]

        def per_group(pieces):
            return attend(pieces[0], pieces[1], pieces[2], pieces[3], visible)
        attended, query_grad, key_grad, value_grad = lax.map(per_group, (split_heads(queries[target], TGT, group_count), split_heads(key_rows, SRC, group_count), split_heads(value_rows, SRC, group_count), split_heads(out_grad[target], TGT, group_count)))
        attended_list.append(merge_heads(attended, TGT))
        query_list.append(merge_heads(query_grad, TGT))

        def add_group(row_total, pieces):
            key_piece, value_piece, key_block, value_block = pieces
            partial_value = jnp.dot(key_piece, key_block.T, preferred_element_type=jnp.float32)
            partial_value = partial_value + jnp.dot(value_piece, value_block.T, preferred_element_type=jnp.float32)
            rounded = lax.optimization_barrier(partial_value.astype(jnp.bfloat16))
            return (row_total + rounded.astype(jnp.float32), None)
        row_total, _ = lax.scan(add_group, jnp.zeros((SRC, D), jnp.float32), (key_grad.reshape(group_count, SRC, group_width), value_grad.reshape(group_count, SRC, group_width), key_blocks, value_blocks))
        row_grad = row_total.astype(jnp.bfloat16)
        grad_list[partner] = norm_backward(enc_states[partner], factor, enc_gain, row_grad)
        key_all = merge_heads(key_grad, SRC)
        value_all = merge_heads(value_grad, SRC)
        key_term = lax.optimization_barrier(jnp.dot(normed.T, key_all, preferred_element_type=jnp.float32).astype(jnp.bfloat16))
        value_term = lax.optimization_barrier(jnp.dot(normed.T, value_all, preferred_element_type=jnp.float32).astype(jnp.bfloat16))
        key_total = key_total + key_term.astype(jnp.float32)
        value_total = value_total + value_term.astype(jnp.float32)
    return (jnp.stack(attended_list), jnp.stack(grad_list), key_total, value_total, jnp.stack(query_list))
```

```python
import functools

import jax
import jax.numpy as jnp
from jax import lax
from jax.experimental import pallas as pl
from jax.experimental.pallas import tpu as pltpu
from jax.sharding import PartitionSpec as P

D = 4096
HD = 256
TGT = 512
ROWS = 128
HALF = 64
QUART = 32
EPS = 1e-06
NEG_FILL = -1e30
MESH = pl.DeviceIdType.MESH
F32 = jnp.float32
BF16 = jnp.bfloat16
VMEM_BYTES = 60 * 1024 * 1024


class Place:
    def __init__(self):
        section, dp, seq = (lax.axis_index(a) for a in ("section", "dp", "seq"))
        self.x, self.y = seq // 4, seq % 4
        self.core = dp % 2
        self.z = section * 2 + dp // 2
        self.position = section * 4 + dp
        x, y, z, core = self.x, self.y, self.z, self.core
        self.ky = y // 2
        self.group = (y % 2 + y // 2) % 2
        self.xp = (section, dp, ((x + 1) % 4) * 4 + y)
        self.xm = (section, dp, ((x + 3) % 4) * 4 + y)
        self.yn = (section, dp, x * 4 + 3 - y)
        self.pair = (section, dp, x * 4 + y + 1 - 2 * (y % 2))
        self.sib = (section, dp + 1 - 2 * core, seq)
        zp, zm = (z + 1) % 4, (z + 3) % 4
        self.zp = (zp // 2, (zp % 2) * 2 + core, seq)
        self.zm = (zm // 2, (zm % 2) * 2 + core, seq)
        self.across = (1 - section, dp, seq)

    def slot(self, dx, w):
        return ((self.x + dx) % 4) * 2 + (self.ky if w == 0 else 1 - self.ky)

    def enter(self):
        everyone = (
            self.xp,
            self.xm,
            self.yn,
            self.pair,
            self.sib,
            self.zp,
            self.zm,
            self.across,
        )
        barrier = pltpu.get_barrier_semaphore()
        for device in everyone:
            pl.semaphore_signal(barrier, inc=1, device_id=device, device_id_type=MESH)
        pl.semaphore_wait(barrier, len(everyone))


def remote(src, dst, send, recv, device):
    return pltpu.make_async_remote_copy(
        src_ref=src,
        dst_ref=dst,
        send_sem=send,
        recv_sem=recv,
        device_id=device,
        device_id_type=MESH,
    )


def at(start, size, unit):
    return pl.ds(pl.multiple_of(start, unit), size)


class Wires:
    def __init__(self, send, recv, home):
        self.send, self.recv, self.home = send, recv, home
        self.open = []

    def put(self, i, src, dst, device):
        copy = remote(src, dst, self.send.at[i], self.recv.at[i], device)
        copy.start()
        self.open.append(copy)

    def got(self, i, dst):
        remote(dst, dst, self.send.at[i], self.recv.at[i], self.home).wait_recv()

    def close(self):
        for copy in self.open:
            copy.wait_send()


GATHER_GOT = (
    (-1, 0, 0, 64),
    (1, 0, 0, 64),
    (2, 0, 0, 32),
    (2, 0, 32, 32),
    (0, 1, 0, 64),
    (-1, 1, 0, 64),
    (1, 1, 0, 64),
    (2, 1, 0, 64),
    (0, 1, 64, 64),
    (-1, 0, 64, 64),
    (1, 0, 64, 64),
    (2, 0, 64, 32),
    (2, 0, 96, 32),
    (-1, 1, 64, 64),
    (1, 1, 64, 64),
    (2, 1, 64, 32),
    (2, 1, 96, 32),
)
GATHER_PUT = (
    (0, 0, 0, 64, "xp"),
    (0, 0, 0, 64, "xm"),
    (-1, 0, 0, 32, "xp"),
    (1, 0, 32, 32, "xm"),
    (0, 0, 0, 64, "yn"),
    (-1, 0, 0, 64, "yn"),
    (1, 0, 0, 64, "yn"),
    (2, 0, 0, 64, "yn"),
    (0, 0, 64, 64, "yn"),
    (0, 0, 64, 64, "xp"),
    (0, 0, 64, 64, "xm"),
    (-1, 0, 64, 32, "xp"),
    (1, 0, 96, 32, "xm"),
    (0, 1, 64, 64, "xp"),
    (0, 1, 64, 64, "xm"),
    (-1, 1, 64, 32, "xp"),
    (1, 1, 96, 32, "xm"),
)


def forward_kernel(
    len_ref, enc, gain, kw, vw, q, g,
    xg_out, wp_out, att, dq, kvg,
    xg, w, wp, kv, kvs, qr, gr, pbuf, sbuf,
    xs, xr, ws, wr, cs, cr, loc,
):
    me = Place()
    load_k = pltpu.make_async_copy(kw, w.at[:, 0:HD], loc.at[0])
    load_v = pltpu.make_async_copy(vw, w.at[:, HD : 2 * HD], loc.at[1])
    load_k.start()
    load_v.start()
    me.enter()

    rows = Wires(xs, xr, me.xp)
    weights = Wires(ws, wr, me.zp)
    heads = Wires(cs, cr, me.pair)

    def piece(spec):
        return xg.at[at(me.slot(spec[0], spec[1]) * ROWS + spec[2], spec[3], 32)]

    def put(*ids):
        for i in ids:
            spec = GATHER_PUT[i]
            rows.put(i, piece(spec), piece(spec), getattr(me, spec[4]))

    def got(*ids):
        for i in ids:
            rows.got(i, piece(GATHER_GOT[i]))

    def slice_of(dz, sibling, first=0, count=512):
        z = (me.z + dz) % 4
        c = 1 - me.core if sibling else me.core
        return wp.at[at((z * 2 + c) * 512 + first, count, 256)]

    mine = me.position * 512
    weights.put(0, kw.at[at(mine, 512, 512)], wp.at[at(mine, 512, 512), 0:HD], me.pair)
    weights.put(1, vw.at[at(mine, 512, 512)], wp.at[at(mine, 512, 512), HD : 2 * HD], me.pair)

    own = me.slot(0, 0) * ROWS

    def norm_rows(i, _):
        wide = enc[at(i * 32, 32, 32), :].astype(F32)
        factor = lax.rsqrt(jnp.mean(wide * wide, axis=-1, keepdims=True) + EPS)
        xg[at(own + i * 32, 32, 32), :] = (wide * factor * gain[...]).astype(BF16)
        return 0

    lax.fori_loop(0, ROWS // 32, norm_rows, 0)
    put(0, 1, 8, 9, 10, 4)

    def project(row, count, matrix, out):
        block = at(row, count, 128)
        out[block, :] = jnp.dot(
            xg[block, :], matrix[...], preferred_element_type=F32
        ).astype(BF16)

    def column(dx):
        return ((me.x + dx) % 4) * 2 * ROWS

    def give_heads(i, row, count):
        block = at(row, count, 128)
        heads.put(i, kvs.at[block], kv.at[at(row + 1024, count, 128)], me.pair)

    weights.got(0, wp.at[at(mine, 512, 512), 0:HD])
    weights.got(1, wp.at[at(mine, 512, 512), HD : 2 * HD])
    weights.put(2, slice_of(0, 0), slice_of(0, 0), me.zp)
    weights.put(3, slice_of(0, 0), slice_of(0, 0), me.zm)
    weights.put(6, slice_of(0, 0), slice_of(0, 0), me.sib)

    got(0)
    put(2, 5)
    got(1)
    put(3, 6)
    got(8)
    put(13, 14)
    weights.got(2, slice_of(-1, 0))
    weights.put(4, slice_of(-1, 0, 0, 256), slice_of(-1, 0, 0, 256), me.zp)
    weights.put(7, slice_of(-1, 0), slice_of(-1, 0), me.sib)
    weights.got(3, slice_of(1, 0))
    weights.put(5, slice_of(1, 0, 256, 256), slice_of(1, 0, 256, 256), me.zm)
    weights.put(8, slice_of(1, 0), slice_of(1, 0), me.sib)
    weights.put(10, q, qr, me.across)
    weights.put(11, g, gr, me.across)
    got(9)
    put(11)
    got(10)
    put(12)
    got(2, 3)
    put(7)
    got(4)
    load_k.wait()
    load_v.wait()
    project(column(0), 256, w, kv)
    weights.got(4, slice_of(2, 0, 0, 256))
    weights.got(5, slice_of(2, 0, 256, 256))
    weights.put(9, slice_of(2, 0), slice_of(2, 0), me.sib)
    for i, dz in enumerate((0, -1, 1, 2)):
        weights.got(6 + i, slice_of(dz, 1))
    keep_w = pltpu.make_async_copy(wp, wp_out, loc.at[2])
    keep_w.start()
    project(column(0), 256, wp, kvs)
    give_heads(0, column(0), 256)
    got(13)
    put(15)
    got(14)
    put(16)
    got(5)
    project(column(-1), 256, wp, kvs)
    give_heads(1, column(-1), 256)
    project(column(-1), 256, w, kv)
    got(6)
    project(column(1), 256, wp, kvs)
    give_heads(2, column(1), 256)
    project(column(1), 256, w, kv)
    got(11, 12)
    far = me.slot(2, 0) * ROWS
    project(far, 128, wp, kvs)
    give_heads(3, far, 128)
    project(far, 128, w, kv)
    got(15, 16, 7)
    last = me.slot(2, 1) * ROWS
    project(last, 128, wp, kvs)
    give_heads(4, last, 128)
    keep_x = pltpu.make_async_copy(xg, xg_out, loc.at[3])
    keep_x.start()
    project(last, 128, w, kv)
    weights.got(10, qr)
    weights.got(11, gr)

    for i, (start, count) in enumerate(
        ((column(0), 256), (column(-1), 256), (column(1), 256), (far, 128), (last, 128))
    ):
        heads.got(i, kv.at[at(start + 1024, count, 128)])

    length = len_ref[me.position]
    lane = lax.broadcasted_iota(jnp.int32, (1, 2048), 1)
    block = (lane % 1024) // ROWS
    group = (me.group + lane // 1024) % 2
    row_y = group + (block % 2) * (3 - 2 * group)
    visible = ((block // 2) * 4 + row_y) * ROWS + lane % ROWS < length
    scale = HD**-0.5
    nt = (((1,), (1,)), ((), ()))
    tn = (((0,), (0,)), ((), ()))

    def attend(i, _):
        part = at(i * 128, 128, 128)
        scores = lax.dot_general(qr[part, :], kv[:, 0:HD], nt, preferred_element_type=F32)
        scores = jnp.where(visible, scores * scale, NEG_FILL)
        top = jnp.max(scores, axis=-1, keepdims=True)
        exponent = jnp.exp(scores - top)
        total = jnp.sum(exponent, axis=-1, keepdims=True)
        probs = exponent * (1.0 / total)
        weights16 = probs.astype(BF16)
        pbuf[part, :] = weights16
        att[part, :] = jnp.dot(
            weights16, kv[:, HD : 2 * HD], preferred_element_type=F32
        ).astype(BF16)
        grad_probs = lax.dot_general(
            gr[part, :], kv[:, HD : 2 * HD], nt, preferred_element_type=F32
        )
        inner = jnp.sum(probs * grad_probs, axis=-1, keepdims=True)
        grad_scores = (probs * (grad_probs - inner) * scale).astype(BF16)
        sbuf[part, :] = grad_scores
        dq[part, :] = jnp.dot(
            grad_scores, kv[:, 0:HD], preferred_element_type=F32
        ).astype(BF16)
        return 0

    lax.fori_loop(0, TGT // 128, attend, 0)

    def transposed(i, _):
        part = at(i * 512, 512, 512)
        kvg[part, 0:HD] = lax.dot_general(
            sbuf[:, part], qr[...], tn, preferred_element_type=F32
        ).astype(BF16)
        kvg[part, HD : 2 * HD] = lax.dot_general(
            pbuf[:, part], gr[...], tn, preferred_element_type=F32
        ).astype(BF16)
        return 0

    lax.fori_loop(0, 4, transposed, 0)

    rows.close()
    weights.close()
    heads.close()
    keep_w.wait()
    keep_x.wait()


Y_TOP = {2: 0, 1: 64, -1: 128, 0: 192}
RINGS = {"top": 256, "low0": 448, "low1": 640}
Y_LOW = 832


def backward_kernel(
    enc, gain, kw, vw, wp_in, xg, kvg, att_in, dq_in,
    enc_grad, kg, vg, att, dq,
    w, wp, x, r, rbuf, kvp, kt, gs, gb, zb, pb, ps, kvv,
    rs, rr, gss, gsr, zs, zr, hs, hr, loc,
):
    me = Place()
    loads = [
        pltpu.make_async_copy(kw, w.at[:, 0:HD], loc.at[0]),
        pltpu.make_async_copy(vw, w.at[:, HD : 2 * HD], loc.at[1]),
        pltpu.make_async_copy(wp_in, wp, loc.at[2]),
        pltpu.make_async_copy(xg, x, loc.at[3]),
    ]
    load_kv = pltpu.make_async_copy(kvg, kvv, loc.at[4])
    load_kv.start()
    for load in loads:
        load.start()
    me.enter()

    rows = Wires(rs, rr, me.xp)
    near = Wires(gss, gsr, me.sib)
    rings = Wires(zs, zr, me.zp)
    heads = Wires(hs, hr, me.pair)
    nt = (((1,), (1,)), ((), ()))

    def column(dx):
        return ((me.x + dx) % 4) * 2 * ROWS

    load_kv.wait()
    order = (2, 1, -1, 0)
    for i, dx in enumerate(order):
        heads.put(
            i,
            kvv.at[at(column(dx) + 1024, 256, 256)],
            kvp.at[at(column(dx), 256, 256)],
            me.pair,
        )
    heads.put(5, att_in, att, me.across)
    heads.put(6, dq_in, dq, me.across)
    kt[0] = kvv[0:1024, :].T
    for load in loads[:3]:
        load.wait()

    def row_terms(dx):
        block = at(column(dx), 256, 256)
        heads.got(order.index(dx), kvp.at[block])

        def tile(n, _):
            cols = at(n * 512, 512, 512)
            total = lax.dot_general(kvv[block, :], w[cols, :], nt, preferred_element_type=F32)
            total += lax.dot_general(kvp[block, :], wp[cols, :], nt, preferred_element_type=F32)
            r[block, cols] = total.astype(BF16)
            return 0

        lax.fori_loop(0, D // 512, tile, 0)

    def rows_of(dx, w_, first, count):
        return at(me.slot(dx, w_) * ROWS + first, count, 32)

    def add(target, source, count):
        def part(i, _):
            to, of = at(target + i * 16, 16, 16), at(source + i * 16, 16, 16)
            r[to, :] = (r[to, :].astype(F32) + rbuf[of, :].astype(F32)).astype(BF16)
            return 0

        lax.fori_loop(0, count // 16, part, 0)

    def y_top(dx):
        i = order.index(dx)
        rows.put(
            i, r.at[rows_of(dx, 1, 0, 64)], rbuf.at[Y_TOP[dx] : Y_TOP[dx] + 64], me.yn
        )

    def y_top_add(dx):
        i = order.index(dx)
        rows.got(i, rbuf.at[Y_TOP[dx] : Y_TOP[dx] + 64])
        add(me.slot(dx, 0) * ROWS, Y_TOP[dx], 64)

    ring_of = {"top": (0, 0, 4), "low0": (0, 64, 8), "low1": (1, 64, 12)}

    def ring_first(name):
        w_, first, i = ring_of[name]
        base = RINGS[name]
        rows.put(i, r.at[rows_of(2, w_, first, 32)], rbuf.at[base : base + 32], me.xp)
        rows.put(
            i + 1, r.at[rows_of(2, w_, first + 32, 32)], rbuf.at[base + 32 : base + 64], me.xm
        )

    def ring_second(name):
        w_, first, i = ring_of[name]
        base = RINGS[name]
        rows.got(i, rbuf.at[base : base + 32])
        add(me.slot(1, w_) * ROWS + first, base, 32)
        rows.put(
            i + 2, r.at[rows_of(1, w_, first, 64)], rbuf.at[base + 64 : base + 128], me.xp
        )
        rows.got(i + 1, rbuf.at[base + 32 : base + 64])
        add(me.slot(-1, w_) * ROWS + first + 32, base + 32, 32)
        rows.put(
            i + 3, r.at[rows_of(-1, w_, first, 64)], rbuf.at[base + 128 : base + 192], me.xm
        )

    def ring_wait(name):
        _, _, i = ring_of[name]
        base = RINGS[name]
        rows.got(i + 2, rbuf.at[base + 64 : base + 128])
        rows.got(i + 3, rbuf.at[base + 128 : base + 192])

    def grad_term(h, dz, sibling):
        z = (me.z + dz) % 4
        c = 1 - me.core if sibling else me.core
        return jnp.dot(
            kt[h], x[:, at((z * 2 + c) * 512, 512, 512)], preferred_element_type=F32
        )

    def near_put(h, n, dz):
        gs[h * 4 + n] = grad_term(h, dz, 1).astype(BF16)
        near.put(h * 4 + n, gs.at[h * 4 + n], gb.at[h * 4 + n], me.sib)

    def near_add(h, n, dz):
        term = grad_term(h, dz, 0)
        near.got(h * 4 + n, gb.at[h * 4 + n])
        gb[h * 4 + n] = (gb[h * 4 + n].astype(F32) + term).astype(BF16)

    def z_first(h):
        rings.put(h * 4, gb.at[h * 4, 0:256], zb.at[h, 0:256], me.zp)
        rings.put(h * 4 + 1, gb.at[h * 4, 256:512], zb.at[h, 256:512], me.zm)

    def z_second(h):
        rings.got(h * 4, zb.at[h, 0:256])
        gb[h * 4 + 1, 0:256] = (
            gb[h * 4 + 1, 0:256].astype(F32) + zb[h, 0:256].astype(F32)
        ).astype(BF16)
        rings.put(h * 4 + 2, gb.at[h * 4 + 1], zb.at[h, 512:1024], me.zp)
        rings.got(h * 4 + 1, zb.at[h, 256:512])
        gb[h * 4 + 2, 256:512] = (
            gb[h * 4 + 2, 256:512].astype(F32) + zb[h, 256:512].astype(F32)
        ).astype(BF16)
        rings.put(h * 4 + 3, gb.at[h * 4 + 2], zb.at[h, 1024:1536], me.zm)

    def z_sum(h):
        rings.got(h * 4 + 2, zb.at[h, 512:1024])
        rings.got(h * 4 + 3, zb.at[h, 1024:1536])
        return (
            gb[h * 4 + 3].astype(F32)
            + zb[h, 512:1024].astype(F32)
            + zb[h, 1024:1536].astype(F32)
        )

    row_terms(2)
    y_top(2)
    ring_first("low1")
    ring_first("low0")
    loads[3].wait()
    near_put(0, 0, 2)
    near_add(0, 0, 2)
    z_first(0)
    row_terms(1)
    y_top(1)
    near_put(0, 1, 1)
    near_put(0, 2, -1)
    row_terms(-1)
    y_top(-1)
    ring_second("low1")
    y_top_add(2)
    ring_first("top")
    near_add(0, 1, 1)
    near_add(0, 2, -1)
    z_second(0)
    row_terms(0)
    y_top(0)
    ring_second("low0")
    near_put(0, 3, 0)
    kt[1] = kvp[...].T
    near_put(1, 0, 2)
    near_put(1, 1, 1)
    near_put(1, 2, -1)
    near_put(1, 3, 0)
    near_add(1, 0, 2)
    z_first(1)
    near_add(0, 3, 0)
    near_add(1, 1, 1)
    near_add(1, 2, -1)
    near_add(1, 3, 0)
    y_top_add(1)
    y_top_add(-1)
    ring_second("top")
    ring_wait("low1")
    base = RINGS["low1"]
    add(me.slot(0, 1) * ROWS + 64, base + 64, 64)
    add(me.slot(0, 1) * ROWS + 64, base + 128, 64)
    rows.put(16, r.at[rows_of(0, 1, 64, 64)], rbuf.at[Y_LOW : Y_LOW + 64], me.yn)
    z_second(1)
    ps[...] = z_sum(1).astype(BF16)
    heads.put(4, ps, pb, me.pair)
    own_sum = z_sum(0)
    heads.got(4, pb)
    total = own_sum + pb[...].astype(F32)
    kg[...] = total[0:HD, :].T
    vg[...] = total[HD : 2 * HD, :].T

    own = me.slot(0, 0) * ROWS
    rows.got(3, rbuf.at[Y_TOP[0] : Y_TOP[0] + 64])
    ring_wait("low0")
    ring_wait("top")
    rows.got(16, rbuf.at[Y_LOW : Y_LOW + 64])

    def finish(first, ring, extra):
        def part(i, _):
            here = at(own + first + i * 16, 16, 16)
            grad = r[here, :].astype(F32)
            for start in (ring + 64, ring + 128, extra):
                grad += rbuf[at(start + i * 16, 16, 16), :].astype(F32)
            out = at(first + i * 16, 16, 16)
            wide = enc[out, :].astype(F32)
            factor = lax.rsqrt(jnp.mean(wide * wide, axis=-1, keepdims=True) + EPS)
            scaled = grad.astype(BF16).astype(F32) * gain[...]
            inner = jnp.mean(scaled * wide, axis=-1, keepdims=True)
            enc_grad[out, :] = (
                factor * scaled - wide * (factor * factor * factor * inner)
            ).astype(BF16)
            return 0

        lax.fori_loop(0, 4, part, 0)

    finish(0, RINGS["top"], Y_TOP[0])
    finish(64, RINGS["low0"], Y_LOW)

    heads.got(5, att)
    heads.got(6, dq)
    rows.close()
    near.close()
    rings.close()
    heads.close()


def on_device(enc_states, enc_gain, key_weight, value_weight, queries, out_grad, lengths):
    enc = enc_states[0]
    gain = enc_gain.reshape(1, D)
    vmem = pl.BlockSpec(memory_space=pltpu.VMEM)
    far = pl.BlockSpec(memory_space=pl.ANY)
    dma = pltpu.SemaphoreType.DMA
    shape = jax.ShapeDtypeStruct

    def params(i):
        return pltpu.CompilerParams(
            collective_id=i, has_side_effects=True, vmem_limit_bytes=VMEM_BYTES
        )

    xg, wp, att, dq, kvg = pl.pallas_call(
        forward_kernel,
        out_shape=(
            shape((1024, D), BF16),
            shape((D, 2 * HD), BF16),
            shape((TGT, HD), BF16),
            shape((TGT, HD), BF16),
            shape((2048, 2 * HD), BF16),
        ),
        in_specs=[pl.BlockSpec(memory_space=pltpu.SMEM), vmem, vmem, far, far, far, far],
        out_specs=(far, far, vmem, vmem, vmem),
        scratch_shapes=[
            pltpu.VMEM((1024, D), BF16),
            pltpu.VMEM((D, 2 * HD), BF16),
            pltpu.VMEM((D, 2 * HD), BF16),
            pltpu.VMEM((2048, 2 * HD), BF16),
            pltpu.VMEM((1024, 2 * HD), BF16),
            pltpu.VMEM((TGT, HD), BF16),
            pltpu.VMEM((TGT, HD), BF16),
            pltpu.VMEM((TGT, 2048), BF16),
            pltpu.VMEM((TGT, 2048), BF16),
            dma((17,)),
            dma((17,)),
            dma((12,)),
            dma((12,)),
            dma((5,)),
            dma((5,)),
            dma((4,)),
        ],
        compiler_params=params(0),
        name="gather_project_attend",
    )(lengths, enc, gain, key_weight, value_weight, queries[0], out_grad[0])

    enc_grad, kg, vg, att, dq = pl.pallas_call(
        backward_kernel,
        out_shape=(
            shape((ROWS, D), BF16),
            shape((512, HD), F32),
            shape((512, HD), F32),
            shape((TGT, HD), BF16),
            shape((TGT, HD), BF16),
        ),
        in_specs=[vmem, vmem] + [far] * 7,
        out_specs=(vmem, vmem, vmem, far, far),
        scratch_shapes=[
            pltpu.VMEM((D, 2 * HD), BF16),
            pltpu.VMEM((D, 2 * HD), BF16),
            pltpu.VMEM((1024, D), BF16),
            pltpu.VMEM((1024, D), BF16),
            pltpu.VMEM((896, D), BF16),
            pltpu.VMEM((1024, 2 * HD), BF16),
            pltpu.VMEM((2, 2 * HD, 1024), BF16),
            pltpu.VMEM((8, 512, 512), BF16),
            pltpu.VMEM((8, 512, 512), BF16),
            pltpu.VMEM((2, 1536, 512), BF16),
            pltpu.VMEM((512, 512), BF16),
            pltpu.VMEM((512, 512), BF16),
            pltpu.VMEM((2048, 2 * HD), BF16),
            dma((17,)),
            dma((17,)),
            dma((8,)),
            dma((8,)),
            dma((8,)),
            dma((8,)),
            dma((7,)),
            dma((7,)),
            dma((5,)),
        ],
        compiler_params=params(1),
        name="row_and_weight_grads",
    )(enc, gain, key_weight, value_weight, wp, xg, kvg, att, dq)
    return (att[None], enc_grad[None], kg, vg, dq[None])


def solution(mesh):
    placed = (
        P(("section", "dp"), "seq", None),
        P(),
        P(None, "seq"),
        P(None, "seq"),
        P(("section", "dp"), None, "seq"),
        P(("section", "dp"), None, "seq"),
        P(),
    )
    return jax.shard_map(
        on_device,
        mesh=mesh,
        in_specs=placed,
        out_specs=(
            P(("section", "dp"), None, "seq"),
            P(("section", "dp"), "seq", None),
            P(("section", "dp"), "seq"),
            P(("section", "dp"), "seq"),
            P(("section", "dp"), None, "seq"),
        ),
        check_vma=False,
    )
```

```python
import jax
import jax.numpy as jnp
from jax import lax
from jax.experimental import pallas as pl
from jax.experimental.pallas import tpu as pltpu
from jax.sharding import PartitionSpec as P

D = 4096
HD = 256
TGT = 512
ROWS = 128
EPS = 1e-06
NEG_FILL = -1e30
MESH = pl.DeviceIdType.MESH
F32 = jnp.float32
BF16 = jnp.bfloat16
VMEM_BYTES = 62 * 1024 * 1024
NT = (((1,), (1,)), ((), ()))
TN = (((0,), (0,)), ((), ()))
CUT = 1792
TOP = (0, CUT)
TOP_A, TOP_B = (0, CUT // 2), (CUT // 2, CUT // 2)
LOW = (CUT, D - CUT)
LOW_A, LOW_B = (CUT, (D - CUT) // 2), (CUT + (D - CUT) // 2, (D - CUT) // 2)


class Place:
    def __init__(self):
        section, dp, seq = (lax.axis_index(a) for a in ("section", "dp", "seq"))
        self.x, self.y = seq // 4, seq % 4
        self.core = dp % 2
        self.z = section * 2 + dp // 2
        self.position = section * 4 + dp
        x, y, z, core = self.x, self.y, self.z, self.core
        self.ky = y // 2
        self.group = (y % 2 + y // 2) % 2
        self.xp = (section, dp, ((x + 1) % 4) * 4 + y)
        self.xm = (section, dp, ((x + 3) % 4) * 4 + y)
        self.yn = (section, dp, x * 4 + 3 - y)
        self.pair = (section, dp, x * 4 + y + 1 - 2 * (y % 2))
        self.sib = (section, dp + 1 - 2 * core, seq)
        zp, zm = (z + 1) % 4, (z + 3) % 4
        self.zp = (zp // 2, (zp % 2) * 2 + core, seq)
        self.zm = (zm // 2, (zm % 2) * 2 + core, seq)
        self.across = (1 - section, dp, seq)

    def column(self, dx):
        return ((self.x + dx) % 4) * 2 * ROWS

    def block(self, dx, w):
        return self.column(dx) + (self.ky if w == 0 else 1 - self.ky) * ROWS

    def enter(self):
        everyone = (
            self.xp,
            self.xm,
            self.yn,
            self.pair,
            self.sib,
            self.zp,
            self.zm,
            self.across,
        )
        barrier = pltpu.get_barrier_semaphore()
        for device in everyone:
            pl.semaphore_signal(barrier, inc=1, device_id=device, device_id_type=MESH)
        pl.semaphore_wait(barrier, len(everyone))


def at(start, size, unit=None):
    return pl.ds(pl.multiple_of(start, unit or min(size, 256)), size)


class Wires:
    def __init__(self, send, recv, home):
        self.send, self.recv, self.home = send, recv, home
        self.open = {}

    def copy(self, i, src, dst, device):
        return pltpu.make_async_remote_copy(
            src_ref=src,
            dst_ref=dst,
            send_sem=self.send.at[i],
            recv_sem=self.recv.at[i],
            device_id=device,
            device_id_type=MESH,
        )

    def put(self, i, src, dst, device):
        self.copy(i, src(), dst(), device).start()
        self.open[i] = src

    def got(self, i, dst):
        self.copy(i, dst(), dst(), self.home).wait_recv()

    def close(self):
        for i, src in self.open.items():
            self.copy(i, src(), src(), self.home).wait_send()


GATHER_GOT = (
    (-1, 0, TOP),
    (1, 0, TOP),
    (2, 0, TOP_A),
    (2, 0, TOP_B),
    (0, 1, TOP),
    (-1, 1, TOP),
    (1, 1, TOP),
    (2, 1, TOP),
    (0, 1, LOW),
    (-1, 0, LOW),
    (1, 0, LOW),
    (2, 0, LOW_A),
    (2, 0, LOW_B),
    (-1, 1, LOW),
    (1, 1, LOW),
    (2, 1, LOW_A),
    (2, 1, LOW_B),
)
GATHER_PUT = (
    (0, 0, TOP, "xp"),
    (0, 0, TOP, "xm"),
    (-1, 0, TOP_A, "xp"),
    (1, 0, TOP_B, "xm"),
    (0, 0, TOP, "yn"),
    (-1, 0, TOP, "yn"),
    (1, 0, TOP, "yn"),
    (2, 0, TOP, "yn"),
    (0, 0, LOW, "yn"),
    (0, 0, LOW, "xp"),
    (0, 0, LOW, "xm"),
    (-1, 0, LOW_A, "xp"),
    (1, 0, LOW_B, "xm"),
    (0, 1, LOW, "xp"),
    (0, 1, LOW, "xm"),
    (-1, 1, LOW_A, "xp"),
    (1, 1, LOW_B, "xm"),
)
ORDER = (2, 1, -1, 0)


def kernel(
    len_ref, enc, gain, kw, vw, q, g,
    row_grad, col_grad, att_out, dq_out,
    xg, w, wp, kv, kvs, qr, gr, pbuf, sbuf, att, dq, kvg, kvp, kt,
    r, yt, ta, tc, la, lc, yl, gb, zb, ps, pb,
    xs, xr, ws, wr, hs, hr, bs, br, ns, nr, zs, zr, loc, gate,
):
    me = Place()
    load_k = pltpu.make_async_copy(kw, w.at[:, 0:HD], loc.at[0])
    load_v = pltpu.make_async_copy(vw, w.at[:, HD : 2 * HD], loc.at[1])
    load_k.start()
    load_v.start()
    me.enter()

    rows = Wires(xs, xr, me.xp)
    weights = Wires(ws, wr, me.zp)
    heads = Wires(hs, hr, me.pair)
    back = Wires(bs, br, me.xp)
    near = Wires(ns, nr, me.sib)
    rings = Wires(zs, zr, me.zp)

    def core(c):
        return pl.when(me.core == c)


    def part(ref, row, cols):
        return lambda: ref.at[at(row(), ROWS), cols[0] : cols[0] + cols[1]]

    def piece(spec):
        return part(xg, lambda: me.block(spec[0], spec[1]), spec[2])

    def put(*ids):
        for i in ids:
            spec = GATHER_PUT[i]
            rows.put(i, piece(spec), piece(spec), getattr(me, spec[3]))

    def got(*ids):
        for i in ids:
            rows.got(i, piece(GATHER_GOT[i]))

    def slice_of(dz, sibling, first=0, count=512):
        z = (me.z + dz) % 4
        c = 1 - me.core if sibling else me.core
        return lambda: wp.at[at((z * 2 + c) * 512 + first, count)]

    def whole(ref):
        return lambda: ref

    mine = me.position * 512
    key_slice = lambda: wp.at[at(mine, 512), 0:HD]
    value_slice = lambda: wp.at[at(mine, 512), HD : 2 * HD]
    weights.put(0, lambda: kw.at[at(mine, 512)], key_slice, me.pair)
    weights.put(1, lambda: vw.at[at(mine, 512)], value_slice, me.pair)
    weights.put(10, whole(q), whole(qr), me.across)
    weights.put(11, whole(g), whole(gr), me.across)

    own = me.block(0, 0)

    def norm_rows(i, _):
        wide = enc[at(i * 32, 32), :].astype(F32)
        factor = lax.rsqrt(jnp.mean(wide * wide, axis=-1, keepdims=True) + EPS)
        xg[at(own + i * 32, 32), :] = (wide * factor * gain[...]).astype(BF16)
        return 0

    lax.fori_loop(0, ROWS // 32, norm_rows, 0)

    def begin():
        put(0, 1, 8, 9, 10, 4)

    def relay_first():
        got(8)
        put(13, 14)
        got(0)
        put(2, 5)
        got(1)
        put(3, 6)

    def relay_second():
        got(9)
        put(11)
        got(10)
        put(12)
        got(2, 3)
        put(7)

    def relay_third():
        got(13)
        put(15)
        got(14)
        put(16)

    @core(0)
    def _():
        begin()
        relay_first()

    weights.got(0, key_slice)
    weights.got(1, value_slice)
    weights.put(2, slice_of(0, 0), slice_of(0, 0), me.zp)
    weights.put(3, slice_of(0, 0), slice_of(0, 0), me.zm)
    weights.put(6, slice_of(0, 0), slice_of(0, 0), me.sib)

    @core(0)
    def _():
        relay_second()
        relay_third()
        pl.semaphore_signal(gate, inc=1, device_id=me.sib, device_id_type=MESH)

    weights.got(2, slice_of(-1, 0))
    weights.put(4, slice_of(-1, 0, 0, 256), slice_of(-1, 0, 0, 256), me.zp)
    weights.put(7, slice_of(-1, 0), slice_of(-1, 0), me.sib)
    weights.got(3, slice_of(1, 0))
    weights.put(5, slice_of(1, 0, 256, 256), slice_of(1, 0, 256, 256), me.zm)
    weights.put(8, slice_of(1, 0), slice_of(1, 0), me.sib)

    @core(1)
    def _():
        pl.semaphore_wait(gate, 1)
        begin()

    weights.got(4, slice_of(2, 0, 0, 256))
    weights.got(5, slice_of(2, 0, 256, 256))
    weights.put(9, slice_of(2, 0), slice_of(2, 0), me.sib)
    load_k.wait()
    load_v.wait()

    @core(1)
    def _():
        relay_first()

    def project(row, count, matrix, out):
        block = at(row, count)
        out[block, :] = jnp.dot(
            xg[block, :], matrix[...], preferred_element_type=F32
        ).astype(BF16)

    def give_heads(i, row, count):
        project(row, count, wp, kvs)
        heads.put(
            i,
            lambda: kvs.at[at(row, count)],
            lambda: kv.at[at(row + 1024, count)],
            me.pair,
        )

    got(4)
    project(me.column(0), 256, w, kv)
    for i, dz in enumerate((0, -1, 1, 2)):
        weights.got(6 + i, slice_of(dz, 1))
    give_heads(0, me.column(0), 256)

    @core(1)
    def _():
        relay_second()
        relay_third()

    got(5)
    give_heads(1, me.column(-1), 256)
    project(me.column(-1), 256, w, kv)
    got(6)
    give_heads(2, me.column(1), 256)
    project(me.column(1), 256, w, kv)
    got(11, 12)
    far = me.block(2, 0)
    give_heads(3, far, 128)
    project(far, 128, w, kv)
    got(15, 16, 7)
    last = me.block(2, 1)
    give_heads(4, last, 128)
    project(last, 128, w, kv)
    weights.got(10, whole(qr))
    weights.got(11, whole(gr))
    given = ((me.column(0), 256), (me.column(-1), 256), (me.column(1), 256), (far, 128), (last, 128))
    for i, (start, count) in enumerate(given):
        heads.got(i, lambda: kv.at[at(start + 1024, count)])


    length = len_ref[me.position]
    lane = lax.broadcasted_iota(jnp.int32, (1, 2048), 1)
    number = (lane % 1024) // ROWS
    group = (me.group + lane // 1024) % 2
    row_y = group + (number % 2) * (3 - 2 * group)
    visible = ((number // 2) * 4 + row_y) * ROWS + lane % ROWS < length
    scale = HD**-0.5

    def attend(i, _):
        here = at(i * 128, 128)
        scores = lax.dot_general(qr[here, :], kv[:, 0:HD], NT, preferred_element_type=F32)
        scores = jnp.where(visible, scores * scale, NEG_FILL)
        top = jnp.max(scores, axis=-1, keepdims=True)
        exponent = jnp.exp(scores - top)
        total = jnp.sum(exponent, axis=-1, keepdims=True)
        probs = exponent * (1.0 / total)
        weights16 = probs.astype(BF16)
        pbuf[here, :] = weights16
        att[here, :] = jnp.dot(
            weights16, kv[:, HD : 2 * HD], preferred_element_type=F32
        ).astype(BF16)
        grad_probs = lax.dot_general(
            gr[here, :], kv[:, HD : 2 * HD], NT, preferred_element_type=F32
        )
        inner = jnp.sum(probs * grad_probs, axis=-1, keepdims=True)
        grad_scores = (probs * (grad_probs - inner) * scale).astype(BF16)
        sbuf[here, :] = grad_scores
        dq[here, :] = jnp.dot(
            grad_scores, kv[:, 0:HD], preferred_element_type=F32
        ).astype(BF16)
        return 0

    lax.fori_loop(0, TGT // 128, attend, 0)

    def head_grads(start):
        here = at(start, 256)
        kvg[here, 0:HD] = lax.dot_general(
            sbuf[:, here], qr[...], TN, preferred_element_type=F32
        ).astype(BF16)
        kvg[here, HD : 2 * HD] = lax.dot_general(
            pbuf[:, here], gr[...], TN, preferred_element_type=F32
        ).astype(BF16)

    def pair_rows(dx):
        return lambda: kvp.at[at(me.column(dx), 256)]

    for i, dx in enumerate(ORDER):
        theirs = me.column(dx) + 1024
        head_grads(theirs)
        heads.put(5 + i, lambda start=theirs: kvg.at[at(start, 256)], pair_rows(dx), me.pair)
    heads.put(9, whole(att), whole(att_out), me.across)
    heads.put(10, whole(dq), whole(dq_out), me.across)
    for dx in ORDER:
        head_grads(me.column(dx))
    kt[0] = kvg[0:1024, :].T


    def row_terms(dx):
        here = at(me.column(dx), 256)
        heads.got(5 + ORDER.index(dx), pair_rows(dx))

        def tile(n, _):
            cols = at(n * 512, 512)
            total = lax.dot_general(kvg[here, :], w[cols, :], NT, preferred_element_type=F32)
            total += lax.dot_general(kvp[here, :], wp[cols, :], NT, preferred_element_type=F32)
            r[here, cols] = total.astype(BF16)
            return 0

        lax.fori_loop(0, D // 512, tile, 0)

    def add(row, cols, source, first=0):
        lo, hi = cols[0], cols[0] + cols[1]

        def some(i, _):
            here = at(row + i * 16, 16)
            came = source()[at(i * 16, 16), first : first + cols[1]]
            r[here, lo:hi] = (r[here, lo:hi].astype(F32) + came.astype(F32)).astype(BF16)
            return 0

        lax.fori_loop(0, ROWS // 16, some, 0)

    def y_top(dx):
        i = ORDER.index(dx)
        back.put(i, part(r, lambda: me.block(dx, 1), TOP), lambda: yt.at[i], me.yn)

    def y_top_add(dx):
        i = ORDER.index(dx)
        back.got(i, lambda: yt.at[i])
        add(me.block(dx, 0), TOP, lambda: yt.at[i])

    ring_of = {
        "top": (0, TOP, TOP_A, TOP_B, 4, lambda: ta, lambda j: tc.at[j]),
        "low0": (0, LOW, LOW_A, LOW_B, 8, lambda: la.at[0], lambda j: lc.at[j]),
        "low1": (1, LOW, LOW_A, LOW_B, 12, lambda: la.at[1], lambda j: lc.at[2 + j]),
    }

    def ring_first(name):
        group_, _, a, b, i, halves, _ = ring_of[name]
        size = a[1]
        back.put(i, part(r, lambda: me.block(2, group_), a), lambda: halves().at[:, 0:size], me.xp)
        back.put(
            i + 1, part(r, lambda: me.block(2, group_), b), lambda: halves().at[:, size : 2 * size], me.xm
        )

    def ring_second(name):
        group_, cols, a, b, i, halves, ends = ring_of[name]
        size = a[1]
        back.got(i, lambda: halves().at[:, 0:size])
        add(me.block(1, group_), a, halves)
        back.put(i + 2, part(r, lambda: me.block(1, group_), cols), lambda: ends(0), me.xp)
        back.got(i + 1, lambda: halves().at[:, size : 2 * size])
        add(me.block(-1, group_), b, halves, size)
        back.put(i + 3, part(r, lambda: me.block(-1, group_), cols), lambda: ends(1), me.xm)

    def ring_wait(name):
        _, _, _, _, i, _, ends = ring_of[name]
        back.got(i + 2, lambda: ends(0))
        back.got(i + 3, lambda: ends(1))


    def grad_term(h, dz, sibling):
        z = (me.z + dz) % 4
        c = 1 - me.core if sibling else me.core
        return jnp.dot(kt[h], xg[:, at((z * 2 + c) * 512, 512)], preferred_element_type=F32)

    staged = (pbuf, sbuf)

    def near_put(h, n):
        src = lambda: staged[h].at[:, n * 512 : (n + 1) * 512]
        staged[h][:, n * 512 : (n + 1) * 512] = grad_term(h, ORDER[n], 1).astype(BF16)
        near.put(h * 4 + n, src, lambda: gb.at[h * 4 + n], me.sib)

    def near_add(h, n):
        term = grad_term(h, ORDER[n], 0)
        near.got(h * 4 + n, lambda: gb.at[h * 4 + n])
        gb[h * 4 + n] = (gb[h * 4 + n].astype(F32) + term).astype(BF16)

    def z_first(h):
        rings.put(h * 6, lambda: gb.at[h * 4, 0:256], lambda: zb.at[h, 0:256], me.zp)
        rings.put(h * 6 + 1, lambda: gb.at[h * 4, 256:512], lambda: zb.at[h, 256:512], me.zm)

    def z_second(h):
        rings.got(h * 6, lambda: zb.at[h, 0:256])
        gb[h * 4 + 1, 0:256] = (
            gb[h * 4 + 1, 0:256].astype(F32) + zb[h, 0:256].astype(F32)
        ).astype(BF16)
        rings.got(h * 6 + 1, lambda: zb.at[h, 256:512])
        gb[h * 4 + 2, 256:512] = (
            gb[h * 4 + 2, 256:512].astype(F32) + zb[h, 256:512].astype(F32)
        ).astype(BF16)
        for j in range(2):
            here = slice(j * 256, j * 256 + 256)
            rings.put(
                h * 6 + 2 + j,
                lambda here=here: gb.at[h * 4 + 1, here],
                lambda j=j: zb.at[h, 512 + j * 256 : 768 + j * 256],
                me.zp,
            )
            rings.put(
                h * 6 + 4 + j,
                lambda here=here: gb.at[h * 4 + 2, here],
                lambda j=j: zb.at[h, 1024 + j * 256 : 1280 + j * 256],
                me.zm,
            )

    def z_sum(h, j):
        first, second = 512 + j * 256, 1024 + j * 256
        rings.got(h * 6 + 2 + j, lambda: zb.at[h, first : first + 256])
        rings.got(h * 6 + 4 + j, lambda: zb.at[h, second : second + 256])
        return (
            gb[h * 4 + 3, j * 256 : j * 256 + 256].astype(F32)
            + zb[h, first : first + 256].astype(F32)
            + zb[h, second : second + 256].astype(F32)
        )

    for n in range(4):
        near_put(0, n)

    @core(1)
    def _():
        near_add(0, 0)
        z_first(0)

    row_terms(2)
    y_top(2)
    ring_first("low1")
    ring_first("low0")

    @core(1)
    def _():
        near_add(0, 1)
        near_add(0, 2)
        z_second(0)

    row_terms(1)
    y_top(1)
    row_terms(-1)
    y_top(-1)
    ring_second("low1")
    y_top_add(2)
    ring_first("top")
    row_terms(0)
    y_top(0)
    kt[1] = kvp[...].T
    for n in range(4):
        near_put(1, n)
    ring_second("low0")

    @core(0)
    def _():
        near_add(0, 0)
        z_first(0)
        near_add(0, 1)
        near_add(0, 2)
        z_second(0)

    near_add(1, 0)
    z_first(1)
    near_add(1, 1)
    near_add(1, 2)
    y_top_add(1)
    y_top_add(-1)
    ring_second("top")
    z_second(1)
    ring_wait("low1")
    add(me.block(0, 1), LOW, lambda: lc.at[2])
    add(me.block(0, 1), LOW, lambda: lc.at[3])
    back.put(16, part(r, lambda: me.block(0, 1), LOW), whole(yl), me.yn)
    near_add(0, 3)
    near_add(1, 3)
    for j in range(2):
        ps[j] = z_sum(1, j).astype(BF16)
        heads.put(11 + j, lambda j=j: ps.at[j], lambda j=j: pb.at[j], me.pair)
    for j in range(2):
        here = slice(j * 256, j * 256 + 256)
        col_grad[here, :] = z_sum(0, j)
    for j in range(2):
        here = slice(j * 256, j * 256 + 256)
        heads.got(11 + j, lambda: pb.at[j])
        col_grad[here, :] += pb[j].astype(F32)

    back.got(3, lambda: yt.at[3])
    ring_wait("low0")
    ring_wait("top")
    back.got(16, whole(yl))

    def finish(cols, *sources):
        lo, hi = cols[0], cols[0] + cols[1]

        def some(i, _):
            grad = r[at(own + i * 16, 16), lo:hi].astype(F32)
            for source in sources:
                grad += source()[at(i * 16, 16), :].astype(F32)
            row_grad[at(i * 16, 16), lo:hi] = grad.astype(BF16)
            return 0

        lax.fori_loop(0, ROWS // 16, some, 0)

    finish(TOP, lambda: tc.at[0], lambda: tc.at[1], lambda: yt.at[3])
    finish(LOW, lambda: lc.at[0], lambda: lc.at[1], whole(yl))

    heads.got(9, whole(att_out))
    heads.got(10, whole(dq_out))
    for wires in (rows, weights, heads, back, near, rings):
        wires.close()


def results_kernel(enc, gain, row_grad, col_grad, att_in, dq_in, enc_grad, kg, vg, att, dq):
    wide = enc[...].astype(F32)
    factor = lax.rsqrt(jnp.mean(wide * wide, axis=-1, keepdims=True) + EPS)
    scaled = row_grad[...].astype(F32) * gain[...]
    inner = jnp.mean(scaled * wide, axis=-1, keepdims=True)
    enc_grad[...] = (factor * scaled - wide * (factor * factor * factor * inner)).astype(BF16)
    kg[...] = col_grad[0:HD, :].T
    vg[...] = col_grad[HD : 2 * HD, :].T
    att[...] = att_in[...]
    dq[...] = dq_in[...]


def on_device(enc_states, enc_gain, key_weight, value_weight, queries, out_grad, lengths):
    enc = enc_states[0]
    gain = enc_gain.reshape(1, D)
    vmem = pl.BlockSpec(memory_space=pltpu.VMEM)
    far = pl.BlockSpec(memory_space=pl.ANY)
    dma = pltpu.SemaphoreType.DMA
    shape = jax.ShapeDtypeStruct
    low = D - CUT

    row_grad, col_grad, att, dq = pl.pallas_call(
        kernel,
        out_shape=(
            shape((ROWS, D), BF16),
            shape((2 * HD, 512), F32),
            shape((TGT, HD), BF16),
            shape((TGT, HD), BF16),
        ),
        in_specs=[pl.BlockSpec(memory_space=pltpu.SMEM), vmem, vmem, far, far, far, far],
        out_specs=(vmem, vmem, far, far),
        scratch_shapes=[
            pltpu.VMEM((1024, D), BF16),
            pltpu.VMEM((D, 2 * HD), BF16),
            pltpu.VMEM((D, 2 * HD), BF16),
            pltpu.VMEM((2048, 2 * HD), BF16),
            pltpu.VMEM((1024, 2 * HD), BF16),
            pltpu.VMEM((TGT, HD), BF16),
            pltpu.VMEM((TGT, HD), BF16),
            pltpu.VMEM((TGT, 2048), BF16),
            pltpu.VMEM((TGT, 2048), BF16),
            pltpu.VMEM((TGT, HD), BF16),
            pltpu.VMEM((TGT, HD), BF16),
            pltpu.VMEM((2048, 2 * HD), BF16),
            pltpu.VMEM((1024, 2 * HD), BF16),
            pltpu.VMEM((2, 2 * HD, 1024), BF16),
            pltpu.VMEM((1024, D), BF16),
            pltpu.VMEM((4, ROWS, CUT), BF16),
            pltpu.VMEM((ROWS, CUT), BF16),
            pltpu.VMEM((2, ROWS, CUT), BF16),
            pltpu.VMEM((2, ROWS, low), BF16),
            pltpu.VMEM((4, ROWS, low), BF16),
            pltpu.VMEM((ROWS, low), BF16),
            pltpu.VMEM((8, 512, 512), BF16),
            pltpu.VMEM((2, 1536, 512), BF16),
            pltpu.VMEM((2, 256, 512), BF16),
            pltpu.VMEM((2, 256, 512), BF16),
            dma((17,)),
            dma((17,)),
            dma((12,)),
            dma((12,)),
            dma((13,)),
            dma((13,)),
            dma((17,)),
            dma((17,)),
            dma((8,)),
            dma((8,)),
            dma((12,)),
            dma((12,)),
            dma((2,)),
            pltpu.SemaphoreType.REGULAR,
        ],
        compiler_params=pltpu.CompilerParams(
            collective_id=0, has_side_effects=True, vmem_limit_bytes=VMEM_BYTES
        ),
        name="gather_attend_scatter",
    )(lengths, enc, gain, key_weight, value_weight, queries[0], out_grad[0])

    def rows_of(count, width):
        return pl.BlockSpec((count, width), lambda i: (i, 0))

    enc_grad, kg, vg, att, dq = pl.pallas_call(
        results_kernel,
        grid=(4,),
        out_shape=(
            shape((ROWS, D), BF16),
            shape((512, HD), F32),
            shape((512, HD), F32),
            shape((TGT, HD), BF16),
            shape((TGT, HD), BF16),
        ),
        in_specs=[
            rows_of(32, D),
            pl.BlockSpec((1, D), lambda i: (0, 0)),
            rows_of(32, D),
            pl.BlockSpec((2 * HD, 128), lambda i: (0, i)),
            rows_of(128, HD),
            rows_of(128, HD),
        ],
        out_specs=(
            rows_of(32, D),
            rows_of(128, HD),
            rows_of(128, HD),
            rows_of(128, HD),
            rows_of(128, HD),
        ),
        name="results",
    )(enc, gain, row_grad, col_grad, att, dq)
    return (att[None], enc_grad[None], kg, vg, dq[None])


def solution(mesh):
    placed = (
        P(("section", "dp"), "seq", None),
        P(),
        P(None, "seq"),
        P(None, "seq"),
        P(("section", "dp"), None, "seq"),
        P(("section", "dp"), None, "seq"),
        P(),
    )
    return jax.shard_map(
        on_device,
        mesh=mesh,
        in_specs=placed,
        out_specs=(
            P(("section", "dp"), None, "seq"),
            P(("section", "dp"), "seq", None),
            P(("section", "dp"), "seq"),
            P(("section", "dp"), "seq"),
            P(("section", "dp"), None, "seq"),
        ),
        check_vma=False,
    )
```

```python
import jax
import jax.numpy as jnp
from jax import lax
from jax.experimental import pallas as pl
from jax.experimental.pallas import tpu as pltpu
from jax.sharding import PartitionSpec as P

D = 4096
HD = 256
TGT = 512
ROWS = 128
EPS = 1e-06
NEG_FILL = -1e30
MESH = pl.DeviceIdType.MESH
F32 = jnp.float32
BF16 = jnp.bfloat16
VMEM_BYTES = 62 * 1024 * 1024
NT = (((1,), (1,)), ((), ()))
TN = (((0,), (0,)), ((), ()))
CUT = 1792
TOP = (0, CUT)
TOP_A, TOP_B = (0, CUT // 2), (CUT // 2, CUT // 2)
LOW = (CUT, D - CUT)
LOW_A, LOW_B = (CUT, (D - CUT) // 2), (CUT + (D - CUT) // 2, (D - CUT) // 2)


class Place:
    def __init__(self):
        section, dp, seq = (lax.axis_index(a) for a in ("section", "dp", "seq"))
        self.x, self.y = seq // 4, seq % 4
        self.core = dp % 2
        self.z = section * 2 + dp // 2
        self.position = section * 4 + dp
        x, y, z, core = self.x, self.y, self.z, self.core
        self.ky = y // 2
        self.group = (y % 2 + y // 2) % 2
        self.xp = (section, dp, ((x + 1) % 4) * 4 + y)
        self.xm = (section, dp, ((x + 3) % 4) * 4 + y)
        self.yn = (section, dp, x * 4 + 3 - y)
        self.pair = (section, dp, x * 4 + y + 1 - 2 * (y % 2))
        self.sib = (section, dp + 1 - 2 * core, seq)
        zp, zm = (z + 1) % 4, (z + 3) % 4
        self.zp = (zp // 2, (zp % 2) * 2 + core, seq)
        self.zm = (zm // 2, (zm % 2) * 2 + core, seq)
        self.across = (1 - section, dp, seq)

    def column(self, dx):
        return ((self.x + dx) % 4) * 2 * ROWS

    def block(self, dx, w):
        return self.column(dx) + (self.ky if w == 0 else 1 - self.ky) * ROWS

    def enter(self, meanwhile):
        everyone = (
            self.xp,
            self.xm,
            self.yn,
            self.pair,
            self.sib,
            self.zp,
            self.zm,
            self.across,
        )
        barrier = pltpu.get_barrier_semaphore()
        for device in everyone:
            pl.semaphore_signal(barrier, inc=1, device_id=device, device_id_type=MESH)
        meanwhile()
        pl.semaphore_wait(barrier, len(everyone))


def at(start, size, unit=None):
    return pl.ds(pl.multiple_of(start, unit or min(size, 256)), size)


class Wires:
    def __init__(self, send, recv, home):
        self.send, self.recv, self.home = send, recv, home
        self.open = {}

    def copy(self, i, src, dst, device):
        return pltpu.make_async_remote_copy(
            src_ref=src,
            dst_ref=dst,
            send_sem=self.send.at[i],
            recv_sem=self.recv.at[i],
            device_id=device,
            device_id_type=MESH,
        )

    def put(self, i, src, dst, device):
        self.copy(i, src(), dst(), device).start()
        self.open[i] = src

    def got(self, i, dst):
        self.copy(i, dst(), dst(), self.home).wait_recv()

    def close(self):
        for i, src in self.open.items():
            self.copy(i, src(), src(), self.home).wait_send()


GATHER_GOT = (
    (-1, 0, TOP),
    (1, 0, TOP),
    (2, 0, TOP_A),
    (2, 0, TOP_B),
    (0, 1, TOP),
    (-1, 1, TOP),
    (1, 1, TOP),
    (2, 1, TOP),
    (0, 1, LOW),
    (-1, 0, LOW),
    (1, 0, LOW),
    (2, 0, LOW_A),
    (2, 0, LOW_B),
    (-1, 1, LOW),
    (1, 1, LOW),
    (2, 1, LOW_A),
    (2, 1, LOW_B),
)
GATHER_PUT = (
    (0, 0, TOP, "xp"),
    (0, 0, TOP, "xm"),
    (-1, 0, TOP_A, "xp"),
    (1, 0, TOP_B, "xm"),
    (0, 0, TOP, "yn"),
    (-1, 0, TOP, "yn"),
    (1, 0, TOP, "yn"),
    (2, 0, TOP, "yn"),
    (0, 0, LOW, "yn"),
    (0, 0, LOW, "xp"),
    (0, 0, LOW, "xm"),
    (-1, 0, LOW_A, "xp"),
    (1, 0, LOW_B, "xm"),
    (0, 1, LOW, "xp"),
    (0, 1, LOW, "xm"),
    (-1, 1, LOW_A, "xp"),
    (1, 1, LOW_B, "xm"),
)
ORDER = (2, 1, -1, 0)
STEPS = (
    "begin@0", "r1@0", "r8@0", "w1K", "w1V", "r0@0", "r10@0", "r9@0", "r13@0", "r23@0", "w2aK",
    "r14@0", "w2bK", "gate@0", "w2aV", "w2bV", "begin@1", "w3K", "w3V", "wallK", "r8@1",
    "wallV", "r0@1", "r1@1", "q", "gV0", "r9@1", "gK0", "o0", "r13@1", "r10@1", "gV-1", "r23@1",
    "r14@1", "gK-1", "gV1", "o1", "gK1", "gate3@1", "gVfar", "ofar", "g", "gVlast", "gKlast",
    "gKfar", "o-1", "olast", "att", "ao", "hgpA", "hgo1", "hgo0", "hgo3", "hgo2", "hgpB",
    "hgp1", "hgp2", "kt0", "hgp3", "np00", "na00@1", "na02@1", "RA", "na01@1", "np02", "RB",
    "zD0@1", "np01", "zC0@1", "R1", "low1C", "R-1", "low1D", "na00@0", "kt1", "np10", "np11",
    "ya2", "R0", "na02@0", "na01@0", "np12", "zD0@0", "zC0@0", "low0D", "low0C", "np03", "ya1",
    "np13", "na10", "yl", "na11", "na12", "na03", "ya-1", "topC", "zs00", "zD1", "zC1", "na13",
    "topD", "zs10", "zs11", "zs01", "pf0", "fin", "pf1",
)


def kernel(
    len_ref, enc, gain, kw, vw, q, g,
    row_grad, col_grad, att_out, dq_out,
    xg, w, wp, kv, kvs, qr, gr, pbuf, sbuf, att, dq, kvg, kvp, kt,
    r, yt, ta, tc, la, lc, yl, gb, zb, ps, pb,
    xs, xr, ws, wr, hs, hr, bs, br, ns, nr, zs, zr, loc, gates,
):
    me = Place()
    load_k = pltpu.make_async_copy(kw, w.at[:, 0:HD], loc.at[0])
    load_v = pltpu.make_async_copy(vw, w.at[:, HD : 2 * HD], loc.at[1])
    load_k.start()
    load_v.start()
    own = me.block(0, 0)

    def norm():
        def some(i, _):
            wide = enc[at(i * 32, 32), :].astype(F32)
            factor = lax.rsqrt(jnp.mean(wide * wide, axis=-1, keepdims=True) + EPS)
            xg[at(own + i * 32, 32), :] = (wide * factor * gain[...]).astype(BF16)
            return 0

        lax.fori_loop(0, ROWS // 32, some, 0)

    me.enter(norm)

    rows = Wires(xs, xr, me.xp)
    weights = Wires(ws, wr, me.zp)
    heads = Wires(hs, hr, me.pair)
    back = Wires(bs, br, me.xp)
    near = Wires(ns, nr, me.sib)
    rings = Wires(zs, zr, me.zp)
    tasks = {}

    def whole(ref):
        return lambda: ref

    def part(ref, row, cols):
        return lambda: ref.at[at(row(), ROWS), cols[0] : cols[0] + cols[1]]


    def piece(spec):
        return part(xg, lambda: me.block(spec[0], spec[1]), spec[2])

    def put(*ids):
        for i in ids:
            spec = GATHER_PUT[i]
            rows.put(i, piece(spec), piece(spec), getattr(me, spec[3]))

    def got(*ids):
        for i in ids:
            rows.got(i, piece(GATHER_GOT[i]))

    def begin():
        @pl.when(me.core == 1)
        def _():
            pl.semaphore_wait(gates.at[0], 1)

        put(0, 1, 8, 9, 10, 4)

    def relay(waits, sends):
        def run():
            got(*waits)
            put(*sends)

        return run

    def signal(i):
        return lambda: pl.semaphore_signal(
            gates.at[i], inc=1, device_id=me.sib, device_id_type=MESH
        )

    tasks["begin"] = begin
    tasks["r8"] = relay((8,), (13, 14))
    tasks["r0"] = relay((0,), (2, 5))
    tasks["r1"] = relay((1,), (3, 6))
    tasks["r9"] = relay((9,), (11,))
    tasks["r10"] = relay((10,), (12,))
    tasks["r23"] = relay((2, 3), (7,))
    tasks["r13"] = relay((13,), (15,))
    tasks["r14"] = relay((14,), (16,))
    tasks["gate"] = signal(0)
    tasks["gate3"] = signal(1)

    for k, kind in enumerate("KV"):

        def one(base, cols, kind):
            def slice_of(dz, sibling, first=0, count=512):
                z = (me.z + dz) % 4
                c = 1 - me.core if sibling else me.core
                start = (z * 2 + c) * 512 + first
                return lambda: wp.at[at(start, count), cols]

            mine, back_, ahead = (slice_of(dz, 0) for dz in (0, -1, 1))
            far, far_a, far_b = (
                slice_of(2, 0),
                slice_of(2, 0, 0, 256),
                slice_of(2, 0, 256, 256),
            )
            others = [slice_of(dz, 1) for dz in (0, -1, 1, 2)]
            back_a, ahead_b = slice_of(-1, 0, 0, 256), slice_of(1, 0, 256, 256)
            source = (kw, vw)[k]
            row = me.position * 512
            weights.put(base, lambda: source.at[at(row, 512)], mine, me.pair)

            def w1():
                weights.got(base, mine)
                weights.put(base + 1, mine, mine, me.zp)
                weights.put(base + 2, mine, mine, me.zm)
                weights.put(base + 5, mine, mine, me.sib)
                if kind == "V":
                    load_k.wait()
                    load_v.wait()

            def w2a():
                weights.got(base + 1, back_)
                weights.put(base + 3, back_a, back_a, me.zp)
                weights.put(base + 6, back_, back_, me.sib)

            def w2b():
                weights.got(base + 2, ahead)
                weights.put(base + 4, ahead_b, ahead_b, me.zm)
                weights.put(base + 7, ahead, ahead, me.sib)

            def w3():
                weights.got(base + 3, far_a)
                weights.got(base + 4, far_b)
                weights.put(base + 8, far, far, me.sib)

            def wall():
                for i in range(4):
                    weights.got(base + 5 + i, others[i])

            tasks["w1" + kind] = w1
            tasks["w2a" + kind] = w2a
            tasks["w2b" + kind] = w2b
            tasks["w3" + kind] = w3
            tasks["wall" + kind] = wall

        one(9 * k, slice(k * HD, k * HD + HD), kind)

    tasks["q"] = lambda: weights.put(18, whole(q), whole(qr), me.across)
    tasks["g"] = lambda: weights.put(19, whole(g), whole(gr), me.across)

    columns = {
        "0": (lambda: me.column(0), 256, (4, 8)),
        "-1": (lambda: me.column(-1), 256, (0, 9, 5, 13)),
        "1": (lambda: me.column(1), 256, (1, 10, 6, 14)),
        "far": (lambda: me.block(2, 0), 128, (2, 3, 11, 12)),
        "last": (lambda: me.block(2, 1), 128, (7, 15, 16)),
    }
    relayed = (8, 0, 1, 9, 10, 2, 3, 13, 14)
    seen = set()

    def project(name, kind):
        start, count, needed = columns[name]
        got(*(i for i in needed if i not in relayed and i not in seen))
        seen.update(needed)
        here = at(start(), count)
        if kind == "o":
            kv[here, :] = jnp.dot(xg[here, :], w[...], preferred_element_type=F32).astype(BF16)
            return
        k = "KV".index(kind)
        cols = slice(k * HD, k * HD + HD)
        kvs[here, cols] = jnp.dot(
            xg[here, :], wp[:, cols], preferred_element_type=F32
        ).astype(BF16)
        heads.put(
            k * 5 + list(columns).index(name),
            lambda: kvs.at[at(start(), count), cols],
            lambda: kv.at[at(start() + 1024, count), cols],
            me.pair,
        )


    def attention():
        for k in range(2):
            for i, (start, count, _) in enumerate(columns.values()):
                heads.got(
                    k * 5 + i,
                    lambda: kv.at[at(start() + 1024, count), k * HD : k * HD + HD],
                )
        weights.got(18, whole(qr))
        weights.got(19, whole(gr))
        length = len_ref[me.position]
        lane = lax.broadcasted_iota(jnp.int32, (1, 2048), 1)
        number = (lane % 1024) // ROWS
        group = (me.group + lane // 1024) % 2
        row_y = group + (number % 2) * (3 - 2 * group)
        visible = ((number // 2) * 4 + row_y) * ROWS + lane % ROWS < length
        scale = HD**-0.5

        def attend(i, _):
            here = at(i * 256, 256)
            scores = lax.dot_general(qr[here, :], kv[:, 0:HD], NT, preferred_element_type=F32)
            scores = jnp.where(visible, scores * scale, NEG_FILL)
            top = jnp.max(scores, axis=-1, keepdims=True)
            exponent = jnp.exp(scores - top)
            total = jnp.sum(exponent, axis=-1, keepdims=True)
            probs = exponent * (1.0 / total)
            weights16 = probs.astype(BF16)
            pbuf[here, :] = weights16
            att[here, :] = jnp.dot(
                weights16, kv[:, HD : 2 * HD], preferred_element_type=F32
            ).astype(BF16)
            grad_probs = lax.dot_general(
                gr[here, :], kv[:, HD : 2 * HD], NT, preferred_element_type=F32
            )
            inner = jnp.sum(probs * grad_probs, axis=-1, keepdims=True)
            grad_scores = (probs * (grad_probs - inner) * scale).astype(BF16)
            sbuf[here, :] = grad_scores
            dq[here, :] = jnp.dot(
                grad_scores, kv[:, 0:HD], preferred_element_type=F32
            ).astype(BF16)
            return 0

        lax.fori_loop(0, TGT // 256, attend, 0, unroll=True)

    tasks["att"] = attention

    def head_grads(start, count):
        here = at(start, count)
        kvg[here, 0:HD] = lax.dot_general(
            sbuf[:, here], qr[...], TN, preferred_element_type=F32
        ).astype(BF16)
        kvg[here, HD : 2 * HD] = lax.dot_general(
            pbuf[:, here], gr[...], TN, preferred_element_type=F32
        ).astype(BF16)

    given = {
        "A": (lambda: me.block(2, 1), 128),
        "B": (lambda: me.block(2, 0), 128),
        "1": (lambda: me.column(1), 256),
        "2": (lambda: me.column(-1), 256),
        "3": (lambda: me.column(0), 256),
    }

    def give_grads(name):
        start, count = given[name]

        def run():
            if name == "1":

                @pl.when(me.core == 0)
                def _():
                    pl.semaphore_wait(gates.at[1], 1)

            head_grads(start() + 1024, count)
            heads.put(
                10 + list(given).index(name),
                lambda: kvg.at[at(start() + 1024, count)],
                lambda: kvp.at[at(start(), count)],
                me.pair,
            )

        return run

    for name in given:
        tasks["hgp" + name] = give_grads(name)
    for i, dx in enumerate(ORDER):
        tasks["hgo%d" % i] = lambda dx=dx: head_grads(me.column(dx), 256)

    def results_back():
        heads.put(15, whole(att), whole(att_out), me.across)
        heads.put(16, whole(dq), whole(dq_out), me.across)

    tasks["ao"] = results_back

    def turn(h):
        kt[h] = (kvg[0:1024, :] if h == 0 else kvp[...]).T


    def got_grads(name):
        if name not in seen:
            seen.add(name)
            start, count = given[name]
            heads.got(10 + list(given).index(name), lambda: kvp.at[at(start(), count)])

    def row_terms(name):
        got_grads(name)
        start, count = given[name]
        here = at(start(), count)

        def tile(n, _):
            cols = at(n * 512, 512)
            total = lax.dot_general(kvg[here, :], w[cols, :], NT, preferred_element_type=F32)
            total += lax.dot_general(kvp[here, :], wp[cols, :], NT, preferred_element_type=F32)
            r[here, cols] = total.astype(BF16)
            return 0

        lax.fori_loop(0, D // 512, tile, 0, unroll=True)
        if name == "A":
            y_top(2)
            ring_first("low1")
        elif name == "B":
            ring_first("low0")
        else:
            y_top({"1": 1, "2": -1, "3": 0}[name])

    def add(row, cols, source, first=0):
        lo, hi = cols[0], cols[0] + cols[1]

        def some(i, _):
            here = at(row + i * 16, 16)
            came = source()[at(i * 16, 16), first : first + cols[1]]
            r[here, lo:hi] = (r[here, lo:hi].astype(F32) + came.astype(F32)).astype(BF16)
            return 0

        lax.fori_loop(0, ROWS // 16, some, 0)

    def y_top(dx):
        i = ORDER.index(dx)
        back.put(i, part(r, lambda: me.block(dx, 1), TOP), lambda: yt.at[i], me.yn)

    def y_top_add(dx):
        i = ORDER.index(dx)
        back.got(i, lambda: yt.at[i])
        add(me.block(dx, 0), TOP, lambda: yt.at[i])
        if dx == 2:
            ring_first("top")

    ring_of = {
        "top": (0, TOP, TOP_A, TOP_B, 4, lambda: ta, lambda j: tc.at[j]),
        "low0": (0, LOW, LOW_A, LOW_B, 8, lambda: la.at[0], lambda j: lc.at[j]),
        "low1": (1, LOW, LOW_A, LOW_B, 12, lambda: la.at[1], lambda j: lc.at[2 + j]),
    }

    def ring_first(name):
        group_, _, a, b, i, halves, _ = ring_of[name]
        size = a[1]
        far = lambda: me.block(2, group_)
        back.put(i, part(r, far, a), lambda: halves().at[:, 0:size], me.xp)
        back.put(i + 1, part(r, far, b), lambda: halves().at[:, size : 2 * size], me.xm)

    def ring_second(name, j):
        group_, cols, a, b, i, halves, ends = ring_of[name]
        size = a[1]
        dx, half, to = ((1, a, me.xp), (-1, b, me.xm))[j]
        back.got(i + j, lambda: halves().at[:, j * size : j * size + size])
        add(me.block(dx, group_), half, halves, j * size)
        back.put(i + 2 + j, part(r, lambda: me.block(dx, group_), cols), lambda: ends(j), to)

    def ring_wait(name):
        _, _, _, _, i, _, ends = ring_of[name]
        back.got(i + 2, lambda: ends(0))
        back.got(i + 3, lambda: ends(1))

    def other_rows():
        ring_wait("low1")
        add(me.block(0, 1), LOW, lambda: lc.at[2])
        add(me.block(0, 1), LOW, lambda: lc.at[3])
        back.put(16, part(r, lambda: me.block(0, 1), LOW), whole(yl), me.yn)

    tasks["yl"] = other_rows
    for dx in (2, 1, -1):
        tasks["ya%d" % dx] = lambda dx=dx: y_top_add(dx)
    for name in ring_of:
        for j in range(2):
            tasks[name + "CD"[j]] = lambda name=name, j=j: ring_second(name, j)


    def grad_term(h, n, sibling):
        z = (me.z + ORDER[n]) % 4
        c = 1 - me.core if sibling else me.core
        return jnp.dot(kt[h], xg[:, at((z * 2 + c) * 512, 512)], preferred_element_type=F32)

    staged = (pbuf, sbuf)

    def near_put(h, n):
        staged[h][:, n * 512 : (n + 1) * 512] = grad_term(h, n, 1).astype(BF16)
        src = lambda: staged[h].at[:, n * 512 : (n + 1) * 512]
        near.put(h * 4 + n, src, lambda: gb.at[h * 4 + n], me.sib)

    def near_add(h, n):
        term = grad_term(h, n, 0)
        near.got(h * 4 + n, lambda: gb.at[h * 4 + n])
        gb[h * 4 + n] = (gb[h * 4 + n].astype(F32) + term).astype(BF16)
        if n == 0:
            lo, hi = slice(0, 256), slice(256, 512)
            rings.put(h * 6, lambda: gb.at[h * 4, lo], lambda: zb.at[h, lo], me.zp)
            rings.put(h * 6 + 1, lambda: gb.at[h * 4, hi], lambda: zb.at[h, hi], me.zm)

    def z_second(h, j):
        half = slice(j * 256, j * 256 + 256)
        chunk = h * 4 + 1 + j
        rings.got(h * 6 + j, lambda: zb.at[h, half])
        gb[chunk, half] = (gb[chunk, half].astype(F32) + zb[h, half].astype(F32)).astype(BF16)
        for i in range(2):
            here = slice(i * 256, i * 256 + 256)
            there = slice(512 * (1 + j) + i * 256, 512 * (1 + j) + i * 256 + 256)
            rings.put(
                h * 6 + 2 + 2 * j + i,
                lambda here=here: gb.at[chunk, here],
                lambda there=there: zb.at[h, there],
                (me.zp, me.zm)[j],
            )

    def z_sum(h, j):
        first, second = 512 + j * 256, 1024 + j * 256
        rings.got(h * 6 + 2 + j, lambda: zb.at[h, first : first + 256])
        rings.got(h * 6 + 4 + j, lambda: zb.at[h, second : second + 256])
        total = (
            gb[h * 4 + 3, j * 256 : j * 256 + 256].astype(F32)
            + zb[h, first : first + 256].astype(F32)
            + zb[h, second : second + 256].astype(F32)
        )
        if h == 0:
            col_grad[j * 256 : j * 256 + 256, :] = total
        else:
            ps[j] = total.astype(BF16)
            heads.put(17 + j, lambda: ps.at[j], lambda: pb.at[j], me.pair)

    def pair_sum(j):
        heads.got(17 + j, lambda: pb.at[j])
        col_grad[j * 256 : j * 256 + 256, :] += pb[j].astype(F32)

    for h in range(2):
        for n in range(4):
            tasks["np%d%d" % (h, n)] = lambda h=h, n=n: near_put(h, n)
            tasks["na%d%d" % (h, n)] = lambda h=h, n=n: near_add(h, n)
        for j in range(2):
            tasks["z%s%d" % ("CD"[j], h)] = lambda h=h, j=j: z_second(h, j)
            tasks["zs%d%d" % (h, j)] = lambda h=h, j=j: z_sum(h, j)
    for j in range(2):
        tasks["pf%d" % j] = lambda j=j: pair_sum(j)


    def finish():
        back.got(3, lambda: yt.at[3])
        ring_wait("low0")
        ring_wait("top")
        back.got(16, whole(yl))

        def total(cols, *sources):
            lo, hi = cols[0], cols[0] + cols[1]

            def some(i, _):
                grad = r[at(own + i * 16, 16), lo:hi].astype(F32)
                for source in sources:
                    grad += source()[at(i * 16, 16), :].astype(F32)
                row_grad[at(i * 16, 16), lo:hi] = grad.astype(BF16)
                return 0

            lax.fori_loop(0, ROWS // 16, some, 0)

        total(TOP, lambda: tc.at[0], lambda: tc.at[1], lambda: yt.at[3])
        total(LOW, lambda: lc.at[0], lambda: lc.at[1], whole(yl))
        heads.got(15, whole(att_out))
        heads.got(16, whole(dq_out))

    tasks["fin"] = finish

    for step in STEPS:
        name, _, only = step.partition("@")

        def run(name=name):
            if name in tasks:
                tasks[name]()
            elif name[0] == "o":
                project(name[1:], "o")
            elif name[0] == "g":
                project(name[2:], name[1])
            elif name == "kt0":
                turn(0)
            elif name == "kt1":
                for each in given:
                    got_grads(each)
                turn(1)
            else:
                row_terms({"RA": "A", "RB": "B", "R1": "1", "R-1": "2", "R0": "3"}[name])

        if only:
            pl.when(me.core == int(only))(run)
        else:
            run()

    for wires in (rows, weights, heads, back, near, rings):
        wires.close()


def results_kernel(enc, gain, row_grad, col_grad, att_in, dq_in, enc_grad, kg, vg, att, dq):
    wide = enc[...].astype(F32)
    factor = lax.rsqrt(jnp.mean(wide * wide, axis=-1, keepdims=True) + EPS)
    scaled = row_grad[...].astype(F32) * gain[...]
    inner = jnp.mean(scaled * wide, axis=-1, keepdims=True)
    enc_grad[...] = (factor * scaled - wide * (factor * factor * factor * inner)).astype(BF16)
    kg[...] = col_grad[0:HD, :].T
    vg[...] = col_grad[HD : 2 * HD, :].T
    att[...] = att_in[...]
    dq[...] = dq_in[...]


def on_device(enc_states, enc_gain, key_weight, value_weight, queries, out_grad, lengths):
    enc = enc_states[0]
    gain = enc_gain.reshape(1, D)
    vmem = pl.BlockSpec(memory_space=pltpu.VMEM)
    far = pl.BlockSpec(memory_space=pl.ANY)
    dma = pltpu.SemaphoreType.DMA
    shape = jax.ShapeDtypeStruct
    low = D - CUT

    row_grad, col_grad, att, dq = pl.pallas_call(
        kernel,
        out_shape=(
            shape((ROWS, D), BF16),
            shape((2 * HD, 512), F32),
            shape((TGT, HD), BF16),
            shape((TGT, HD), BF16),
        ),
        in_specs=[pl.BlockSpec(memory_space=pltpu.SMEM), vmem, vmem, far, far, far, far],
        out_specs=(vmem, vmem, far, far),
        scratch_shapes=[
            pltpu.VMEM((1024, D), BF16),
            pltpu.VMEM((D, 2 * HD), BF16),
            pltpu.VMEM((D, 2 * HD), BF16),
            pltpu.VMEM((2048, 2 * HD), BF16),
            pltpu.VMEM((1024, 2 * HD), BF16),
            pltpu.VMEM((TGT, HD), BF16),
            pltpu.VMEM((TGT, HD), BF16),
            pltpu.VMEM((TGT, 2048), BF16),
            pltpu.VMEM((TGT, 2048), BF16),
            pltpu.VMEM((TGT, HD), BF16),
            pltpu.VMEM((TGT, HD), BF16),
            pltpu.VMEM((2048, 2 * HD), BF16),
            pltpu.VMEM((1024, 2 * HD), BF16),
            pltpu.VMEM((2, 2 * HD, 1024), BF16),
            pltpu.VMEM((1024, D), BF16),
            pltpu.VMEM((4, ROWS, CUT), BF16),
            pltpu.VMEM((ROWS, CUT), BF16),
            pltpu.VMEM((2, ROWS, CUT), BF16),
            pltpu.VMEM((2, ROWS, low), BF16),
            pltpu.VMEM((4, ROWS, low), BF16),
            pltpu.VMEM((ROWS, low), BF16),
            pltpu.VMEM((8, 512, 512), BF16),
            pltpu.VMEM((2, 1536, 512), BF16),
            pltpu.VMEM((2, 256, 512), BF16),
            pltpu.VMEM((2, 256, 512), BF16),
            dma((17,)),
            dma((17,)),
            dma((20,)),
            dma((20,)),
            dma((19,)),
            dma((19,)),
            dma((17,)),
            dma((17,)),
            dma((8,)),
            dma((8,)),
            dma((12,)),
            dma((12,)),
            dma((2,)),
            pltpu.SemaphoreType.REGULAR((2,)),
        ],
        compiler_params=pltpu.CompilerParams(
            collective_id=0, has_side_effects=True, vmem_limit_bytes=VMEM_BYTES
        ),
        name="gather_attend_scatter",
    )(lengths, enc, gain, key_weight, value_weight, queries[0], out_grad[0])

    def rows_of(count, width):
        return pl.BlockSpec((count, width), lambda i: (i, 0))

    enc_grad, kg, vg, att, dq = pl.pallas_call(
        results_kernel,
        grid=(2,),
        out_shape=(
            shape((ROWS, D), BF16),
            shape((512, HD), F32),
            shape((512, HD), F32),
            shape((TGT, HD), BF16),
            shape((TGT, HD), BF16),
        ),
        in_specs=[
            rows_of(64, D),
            pl.BlockSpec((1, D), lambda i: (0, 0)),
            rows_of(64, D),
            pl.BlockSpec((2 * HD, 256), lambda i: (0, i)),
            rows_of(256, HD),
            rows_of(256, HD),
        ],
        out_specs=(
            rows_of(64, D),
            rows_of(256, HD),
            rows_of(256, HD),
            rows_of(256, HD),
            rows_of(256, HD),
        ),
        name="results",
    )(enc, gain, row_grad, col_grad, att, dq)
    return (att[None], enc_grad[None], kg, vg, dq[None])


def solution(mesh):
    placed = (
        P(("section", "dp"), "seq", None),
        P(),
        P(None, "seq"),
        P(None, "seq"),
        P(("section", "dp"), None, "seq"),
        P(("section", "dp"), None, "seq"),
        P(),
    )
    return jax.shard_map(
        on_device,
        mesh=mesh,
        in_specs=placed,
        out_specs=(
            P(("section", "dp"), None, "seq"),
            P(("section", "dp"), "seq", None),
            P(("section", "dp"), "seq"),
            P(("section", "dp"), "seq"),
            P(("section", "dp"), None, "seq"),
        ),
        check_vma=False,
    )
```

```python
import jax
import jax.numpy as jnp
from jax import lax
from jax.experimental import pallas as pl
from jax.experimental.pallas import tpu as pltpu
from jax.sharding import PartitionSpec as P

D = 4096
HD = 256
TGT = 512
ROWS = 128
EPS = 1e-06
NEG_FILL = -1e30
MESH = pl.DeviceIdType.MESH
F32 = jnp.float32
BF16 = jnp.bfloat16
VMEM_BYTES = 62 * 1024 * 1024
NT = (((1,), (1,)), ((), ()))
TN = (((0,), (0,)), ((), ()))
CUT = 1792
TOP = (0, CUT)
TOP_A, TOP_B = (0, CUT // 2), (CUT // 2, CUT // 2)
LOW = (CUT, D - CUT)
LOW_A, LOW_B = (CUT, (D - CUT) // 2), (CUT + (D - CUT) // 2, (D - CUT) // 2)


class Place:
    def __init__(self):
        section, dp, seq = (lax.axis_index(a) for a in ("section", "dp", "seq"))
        self.x, self.y = seq // 4, seq % 4
        self.core = dp % 2
        self.z = section * 2 + dp // 2
        self.position = section * 4 + dp
        x, y, z, core = self.x, self.y, self.z, self.core
        self.ky = y // 2
        self.group = (y % 2 + y // 2) % 2
        self.xp = (section, dp, ((x + 1) % 4) * 4 + y)
        self.xm = (section, dp, ((x + 3) % 4) * 4 + y)
        self.yn = (section, dp, x * 4 + 3 - y)
        self.pair = (section, dp, x * 4 + y + 1 - 2 * (y % 2))
        self.sib = (section, dp + 1 - 2 * core, seq)
        zp, zm = (z + 1) % 4, (z + 3) % 4
        self.zp = (zp // 2, (zp % 2) * 2 + core, seq)
        self.zm = (zm // 2, (zm % 2) * 2 + core, seq)
        self.across = (1 - section, dp, seq)

    def column(self, dx):
        return ((self.x + dx) % 4) * 2 * ROWS

    def block(self, dx, w):
        return self.column(dx) + (self.ky if w == 0 else 1 - self.ky) * ROWS

    def enter(self, meanwhile):
        everyone = (
            self.xp,
            self.xm,
            self.yn,
            self.pair,
            self.sib,
            self.zp,
            self.zm,
            self.across,
        )
        barrier = pltpu.get_barrier_semaphore()
        for device in everyone:
            pl.semaphore_signal(barrier, inc=1, device_id=device, device_id_type=MESH)
        meanwhile()
        pl.semaphore_wait(barrier, len(everyone))


def at(start, size, unit=None):
    return pl.ds(pl.multiple_of(start, unit or min(size, 256)), size)


class Wires:
    def __init__(self, send, recv, home):
        self.send, self.recv, self.home = send, recv, home
        self.open = {}

    def copy(self, i, src, dst, device):
        return pltpu.make_async_remote_copy(
            src_ref=src,
            dst_ref=dst,
            send_sem=self.send.at[i],
            recv_sem=self.recv.at[i],
            device_id=device,
            device_id_type=MESH,
        )

    def put(self, i, src, dst, device):
        self.copy(i, src(), dst(), device).start()
        self.open[i] = src

    def got(self, i, dst):
        self.copy(i, dst(), dst(), self.home).wait_recv()

    def close(self, ids=None):
        for i in list(self.open) if ids is None else ids:
            src = self.open.pop(i)
            self.copy(i, src(), src(), self.home).wait_send()


GATHER_GOT = (
    (-1, 0, TOP),
    (1, 0, TOP),
    (2, 0, TOP_A),
    (2, 0, TOP_B),
    (0, 1, TOP),
    (-1, 1, TOP),
    (1, 1, TOP),
    (2, 1, TOP),
    (0, 1, LOW),
    (-1, 0, LOW),
    (1, 0, LOW),
    (2, 0, LOW_A),
    (2, 0, LOW_B),
    (-1, 1, LOW),
    (1, 1, LOW),
    (2, 1, LOW_A),
    (2, 1, LOW_B),
)
GATHER_PUT = (
    (0, 0, TOP, "xp"),
    (0, 0, TOP, "xm"),
    (-1, 0, TOP_A, "xp"),
    (1, 0, TOP_B, "xm"),
    (0, 0, TOP, "yn"),
    (-1, 0, TOP, "yn"),
    (1, 0, TOP, "yn"),
    (2, 0, TOP, "yn"),
    (0, 0, LOW, "yn"),
    (0, 0, LOW, "xp"),
    (0, 0, LOW, "xm"),
    (-1, 0, LOW_A, "xp"),
    (1, 0, LOW_B, "xm"),
    (0, 1, LOW, "xp"),
    (0, 1, LOW, "xm"),
    (-1, 1, LOW_A, "xp"),
    (1, 1, LOW_B, "xm"),
)
ORDER = (2, 1, -1, 0)
STEPS = (
    "begin@0", "r1@0", "r8@0", "w1K", "w1V", "r0@0", "r10@0", "r9@0", "r13@0", "r23@0", "w2aK",
    "r14@0", "w2bK", "gate@0", "w2aV", "w2bV", "begin@1", "gate3@1", "w3K", "w3V", "wallK",
    "r8@1", "wallV", "r0@1", "r1@1", "q", "gV0", "r9@1", "gK0", "o0", "r13@1", "r10@1", "gV-1",
    "r23@1", "r14@1", "gK-1", "gV1", "o1", "gK1", "gVfar", "ofar", "g", "gVlast", "gKlast",
    "gKfar", "o-1", "olast", "att", "hgpA", "hgo1", "hgo0", "hgo3", "hgo2", "hgpB", "hgp1",
    "hgp2", "kt0", "hgp3", "ao@0", "ad@0", "np00", "na00@1", "na02@1", "RA", "na01@1", "np02",
    "RB", "zD0@1", "np01", "zC0@1", "R1", "low1C", "R-1", "low1D", "na00@0", "kt1", "np10",
    "np11", "ya2", "R0", "na02@0", "na01@0", "np12", "zD0@0", "zC0@0", "low0D", "low0C", "np03",
    "ya1", "np13", "na10", "yl", "na11", "na12", "na03", "ya-1", "topC", "zs00", "zD1", "zC1",
    "ao@1", "ad@1", "na13", "topD", "zs10", "zs11", "zs01", "pf0", "fin", "pf1",
)


def kernel(
    len_ref, enc, gain, kw, vw, q, g,
    row_grad, col_grad, att_out, dq_out,
    xg, w, wp, kv, kvs, qr, gr, pbuf, sbuf, att, dq, kvg, kvp, kt,
    r, yt, ta, tc, la, lc, yl, gb, zb, ps, pb, rg, cg,
    xs, xr, ws, wr, hs, hr, bs, br, ns, nr, zs, zr, loc, gates,
):
    me = Place()
    load_k = pltpu.make_async_copy(kw, w.at[:, 0:HD], loc.at[0])
    load_v = pltpu.make_async_copy(vw, w.at[:, HD : 2 * HD], loc.at[1])
    load_k.start()
    load_v.start()
    own = me.block(0, 0)

    def norm():
        def some(i, _):
            wide = enc[at(i * 32, 32), :].astype(F32)
            factor = lax.rsqrt(jnp.mean(wide * wide, axis=-1, keepdims=True) + EPS)
            xg[at(own + i * 32, 32), :] = (wide * factor * gain[...]).astype(BF16)
            return 0

        lax.fori_loop(0, ROWS // 32, some, 0)

    me.enter(norm)

    rows = Wires(xs, xr, me.xp)
    weights = Wires(ws, wr, me.zp)
    heads = Wires(hs, hr, me.pair)
    back = Wires(bs, br, me.xp)
    near = Wires(ns, nr, me.sib)
    rings = Wires(zs, zr, me.zp)
    tasks = {}

    def whole(ref):
        return lambda: ref

    def part(ref, row, cols):
        return lambda: ref.at[at(row(), ROWS), cols[0] : cols[0] + cols[1]]


    def piece(spec):
        return part(xg, lambda: me.block(spec[0], spec[1]), spec[2])

    def put(*ids):
        for i in ids:
            spec = GATHER_PUT[i]
            rows.put(i, piece(spec), piece(spec), getattr(me, spec[3]))

    def got(*ids):
        for i in ids:
            rows.got(i, piece(GATHER_GOT[i]))

    def begin():
        @pl.when(me.core == 1)
        def _():
            pl.semaphore_wait(gates.at[0], 1)

        put(0, 1, 8, 9, 10, 4)

    def relay(waits, sends):
        def run():
            got(*waits)
            put(*sends)

        return run

    def signal(i):
        return lambda: pl.semaphore_signal(
            gates.at[i], inc=1, device_id=me.sib, device_id_type=MESH
        )

    tasks["begin"] = begin
    tasks["r8"] = relay((8,), (13, 14))
    tasks["r0"] = relay((0,), (2, 5))
    tasks["r1"] = relay((1,), (3, 6))
    tasks["r9"] = relay((9,), (11,))
    tasks["r10"] = relay((10,), (12,))
    tasks["r23"] = relay((2, 3), (7,))
    tasks["r13"] = relay((13,), (15,))
    tasks["r14"] = relay((14,), (16,))
    tasks["gate"] = signal(0)
    tasks["gate3"] = signal(1)

    for k, kind in enumerate("KV"):

        def one(base, cols, kind):
            def slice_of(dz, sibling, first=0, count=512):
                z = (me.z + dz) % 4
                c = 1 - me.core if sibling else me.core
                start = (z * 2 + c) * 512 + first
                return lambda: wp.at[at(start, count), cols]

            mine, back_, ahead = (slice_of(dz, 0) for dz in (0, -1, 1))
            far, far_a, far_b = (
                slice_of(2, 0),
                slice_of(2, 0, 0, 256),
                slice_of(2, 0, 256, 256),
            )
            others = [slice_of(dz, 1) for dz in (0, -1, 1, 2)]
            back_a, ahead_b = slice_of(-1, 0, 0, 256), slice_of(1, 0, 256, 256)
            source = (kw, vw)[k]
            row = me.position * 512
            weights.put(base, lambda: source.at[at(row, 512)], mine, me.pair)

            def w1():
                weights.got(base, mine)
                weights.put(base + 1, mine, mine, me.zp)
                weights.put(base + 2, mine, mine, me.zm)
                weights.put(base + 5, mine, mine, me.sib)
                if kind == "V":
                    load_k.wait()
                    load_v.wait()

            def w2a():
                weights.got(base + 1, back_)
                weights.put(base + 3, back_a, back_a, me.zp)
                weights.put(base + 6, back_, back_, me.sib)

            def w2b():
                weights.got(base + 2, ahead)
                weights.put(base + 4, ahead_b, ahead_b, me.zm)
                weights.put(base + 7, ahead, ahead, me.sib)

            def w3():
                weights.got(base + 3, far_a)
                weights.got(base + 4, far_b)
                weights.put(base + 8, far, far, me.sib)

            def wall():
                for i in range(4):
                    weights.got(base + 5 + i, others[i])

            tasks["w1" + kind] = w1
            tasks["w2a" + kind] = w2a
            tasks["w2b" + kind] = w2b
            tasks["w3" + kind] = w3
            tasks["wall" + kind] = wall

        one(9 * k, slice(k * HD, k * HD + HD), kind)

    tasks["q"] = lambda: weights.put(18, whole(q), whole(qr), me.across)
    tasks["g"] = lambda: weights.put(19, whole(g), whole(gr), me.across)

    columns = {
        "0": (lambda: me.column(0), 256, (4, 8)),
        "-1": (lambda: me.column(-1), 256, (0, 9, 5, 13)),
        "1": (lambda: me.column(1), 256, (1, 10, 6, 14)),
        "far": (lambda: me.block(2, 0), 128, (2, 3, 11, 12)),
        "last": (lambda: me.block(2, 1), 128, (7, 15, 16)),
    }
    relayed = (8, 0, 1, 9, 10, 2, 3, 13, 14)
    seen = set()

    def project(name, kind):
        start, count, needed = columns[name]
        got(*(i for i in needed if i not in relayed and i not in seen))
        seen.update(needed)
        here = at(start(), count)
        if kind == "o":
            kv[here, :] = jnp.dot(xg[here, :], w[...], preferred_element_type=F32).astype(BF16)
            return
        k = "KV".index(kind)
        cols = slice(k * HD, k * HD + HD)
        kvs[here, cols] = jnp.dot(
            xg[here, :], wp[:, cols], preferred_element_type=F32
        ).astype(BF16)
        heads.put(
            k * 5 + list(columns).index(name),
            lambda: kvs.at[at(start(), count), cols],
            lambda: kv.at[at(start() + 1024, count), cols],
            me.pair,
        )


    def attention():
        for k in range(2):
            for i, (start, count, _) in enumerate(columns.values()):
                heads.got(
                    k * 5 + i,
                    lambda: kv.at[at(start() + 1024, count), k * HD : k * HD + HD],
                )
        weights.got(18, whole(qr))
        weights.got(19, whole(gr))
        length = len_ref[me.position]
        lane = lax.broadcasted_iota(jnp.int32, (1, 2048), 1)
        number = (lane % 1024) // ROWS
        group = (me.group + lane // 1024) % 2
        row_y = group + (number % 2) * (3 - 2 * group)
        visible = ((number // 2) * 4 + row_y) * ROWS + lane % ROWS < length
        scale = HD**-0.5

        def attend(i, _):
            here = at(i * 256, 256)
            scores = lax.dot_general(qr[here, :], kv[:, 0:HD], NT, preferred_element_type=F32)
            scores = jnp.where(visible, scores * scale, NEG_FILL)
            top = jnp.max(scores, axis=-1, keepdims=True)
            exponent = jnp.exp(scores - top)
            total = jnp.sum(exponent, axis=-1, keepdims=True)
            probs = exponent * (1.0 / total)
            weights16 = probs.astype(BF16)
            pbuf[here, :] = weights16
            att[here, :] = jnp.dot(
                weights16, kv[:, HD : 2 * HD], preferred_element_type=F32
            ).astype(BF16)
            grad_probs = lax.dot_general(
                gr[here, :], kv[:, HD : 2 * HD], NT, preferred_element_type=F32
            )
            inner = jnp.sum(probs * grad_probs, axis=-1, keepdims=True)
            grad_scores = (probs * (grad_probs - inner) * scale).astype(BF16)
            sbuf[here, :] = grad_scores
            dq[here, :] = jnp.dot(
                grad_scores, kv[:, 0:HD], preferred_element_type=F32
            ).astype(BF16)
            return 0

        lax.fori_loop(0, TGT // 256, attend, 0, unroll=True)

    tasks["att"] = attention

    def head_grads(start, count):
        here = at(start, count)
        kvg[here, 0:HD] = lax.dot_general(
            sbuf[:, here], qr[...], TN, preferred_element_type=F32
        ).astype(BF16)
        kvg[here, HD : 2 * HD] = lax.dot_general(
            pbuf[:, here], gr[...], TN, preferred_element_type=F32
        ).astype(BF16)

    given = {
        "A": (lambda: me.block(2, 1), 128),
        "B": (lambda: me.block(2, 0), 128),
        "1": (lambda: me.column(1), 256),
        "2": (lambda: me.column(-1), 256),
        "3": (lambda: me.column(0), 256),
    }

    def give_grads(name):
        start, count = given[name]

        def run():
            if name == "1":

                @pl.when(me.core == 0)
                def _():
                    pl.semaphore_wait(gates.at[1], 1)

            head_grads(start() + 1024, count)
            heads.put(
                10 + list(given).index(name),
                lambda: kvg.at[at(start() + 1024, count)],
                lambda: kvp.at[at(start(), count)],
                me.pair,
            )

        return run

    for name in given:
        tasks["hgp" + name] = give_grads(name)
    for i, dx in enumerate(ORDER):
        tasks["hgo%d" % i] = lambda dx=dx: head_grads(me.column(dx), 256)

    tasks["ao"] = lambda: heads.put(15, whole(att), whole(att_out), me.across)
    tasks["ad"] = lambda: heads.put(16, whole(dq), whole(dq_out), me.across)

    def turn(h):
        kt[h] = (kvg[0:1024, :] if h == 0 else kvp[...]).T


    def got_grads(name):
        if name not in seen:
            seen.add(name)
            start, count = given[name]
            heads.got(10 + list(given).index(name), lambda: kvp.at[at(start(), count)])

    def row_terms(name):
        got_grads(name)
        start, count = given[name]
        here = at(start(), count)

        def tile(n, _):
            cols = at(n * 512, 512)
            total = lax.dot_general(kvg[here, :], w[cols, :], NT, preferred_element_type=F32)
            total += lax.dot_general(kvp[here, :], wp[cols, :], NT, preferred_element_type=F32)
            r[here, cols] = total.astype(BF16)
            return 0

        lax.fori_loop(0, D // 512, tile, 0, unroll=True)
        if name == "A":
            y_top(2)
            ring_first("low1")
        elif name == "B":
            ring_first("low0")
        else:
            y_top({"1": 1, "2": -1, "3": 0}[name])

    def add(row, cols, source, first=0):
        lo, hi = cols[0], cols[0] + cols[1]

        def some(i, _):
            here = at(row + i * 16, 16)
            came = source()[at(i * 16, 16), first : first + cols[1]]
            r[here, lo:hi] = (r[here, lo:hi].astype(F32) + came.astype(F32)).astype(BF16)
            return 0

        lax.fori_loop(0, ROWS // 16, some, 0)

    def y_top(dx):
        i = ORDER.index(dx)
        back.put(i, part(r, lambda: me.block(dx, 1), TOP), lambda: yt.at[i], me.yn)

    def y_top_add(dx):
        i = ORDER.index(dx)
        back.got(i, lambda: yt.at[i])
        add(me.block(dx, 0), TOP, lambda: yt.at[i])
        if dx == 2:
            ring_first("top")

    ring_of = {
        "top": (0, TOP, TOP_A, TOP_B, 4, lambda: ta, lambda j: tc.at[j]),
        "low0": (0, LOW, LOW_A, LOW_B, 8, lambda: la.at[0], lambda j: lc.at[j]),
        "low1": (1, LOW, LOW_A, LOW_B, 12, lambda: la.at[1], lambda j: lc.at[2 + j]),
    }

    def ring_first(name):
        group_, _, a, b, i, halves, _ = ring_of[name]
        size = a[1]
        far = lambda: me.block(2, group_)
        back.put(i, part(r, far, a), lambda: halves().at[:, 0:size], me.xp)
        back.put(i + 1, part(r, far, b), lambda: halves().at[:, size : 2 * size], me.xm)

    def ring_second(name, j):
        group_, cols, a, b, i, halves, ends = ring_of[name]
        size = a[1]
        dx, half, to = ((1, a, me.xp), (-1, b, me.xm))[j]
        back.got(i + j, lambda: halves().at[:, j * size : j * size + size])
        add(me.block(dx, group_), half, halves, j * size)
        back.put(i + 2 + j, part(r, lambda: me.block(dx, group_), cols), lambda: ends(j), to)

    def ring_wait(name):
        _, _, _, _, i, _, ends = ring_of[name]
        back.got(i + 2, lambda: ends(0))
        back.got(i + 3, lambda: ends(1))

    def other_rows():
        ring_wait("low1")
        add(me.block(0, 1), LOW, lambda: lc.at[2])
        add(me.block(0, 1), LOW, lambda: lc.at[3])
        back.put(16, part(r, lambda: me.block(0, 1), LOW), whole(yl), me.yn)

    tasks["yl"] = other_rows
    for dx in (2, 1, -1):
        tasks["ya%d" % dx] = lambda dx=dx: y_top_add(dx)
    for name in ring_of:
        for j in range(2):
            tasks[name + "CD"[j]] = lambda name=name, j=j: ring_second(name, j)


    def grad_term(h, n, sibling):
        z = (me.z + ORDER[n]) % 4
        c = 1 - me.core if sibling else me.core
        return jnp.dot(kt[h], xg[:, at((z * 2 + c) * 512, 512)], preferred_element_type=F32)

    staged = (pbuf, sbuf)

    def near_put(h, n):
        staged[h][:, n * 512 : (n + 1) * 512] = grad_term(h, n, 1).astype(BF16)
        src = lambda: staged[h].at[:, n * 512 : (n + 1) * 512]
        near.put(h * 4 + n, src, lambda: gb.at[h * 4 + n], me.sib)

    def near_add(h, n):
        term = grad_term(h, n, 0)
        near.got(h * 4 + n, lambda: gb.at[h * 4 + n])
        gb[h * 4 + n] = (gb[h * 4 + n].astype(F32) + term).astype(BF16)
        if n == 0:
            lo, hi = slice(0, 256), slice(256, 512)
            rings.put(h * 6, lambda: gb.at[h * 4, lo], lambda: zb.at[h, lo], me.zp)
            rings.put(h * 6 + 1, lambda: gb.at[h * 4, hi], lambda: zb.at[h, hi], me.zm)

    def z_second(h, j):
        half = slice(j * 256, j * 256 + 256)
        chunk = h * 4 + 1 + j
        rings.got(h * 6 + j, lambda: zb.at[h, half])
        gb[chunk, half] = (gb[chunk, half].astype(F32) + zb[h, half].astype(F32)).astype(BF16)
        for i in range(2):
            here = slice(i * 256, i * 256 + 256)
            there = slice(512 * (1 + j) + i * 256, 512 * (1 + j) + i * 256 + 256)
            rings.put(
                h * 6 + 2 + 2 * j + i,
                lambda here=here: gb.at[chunk, here],
                lambda there=there: zb.at[h, there],
                (me.zp, me.zm)[j],
            )

    def z_sum(h, j):
        first, second = 512 + j * 256, 1024 + j * 256
        rings.got(h * 6 + 2 + j, lambda: zb.at[h, first : first + 256])
        rings.got(h * 6 + 4 + j, lambda: zb.at[h, second : second + 256])
        total = (
            gb[h * 4 + 3, j * 256 : j * 256 + 256].astype(F32)
            + zb[h, first : first + 256].astype(F32)
            + zb[h, second : second + 256].astype(F32)
        )
        if h == 0:
            cg[j * 256 : j * 256 + 256, :] = total
        else:
            ps[j] = total.astype(BF16)
            heads.put(17 + j, lambda: ps.at[j], lambda: pb.at[j], me.pair)

    def col_out(j):
        half = slice(j * 256, j * 256 + 256)
        return pltpu.make_async_copy(cg.at[half], col_grad.at[half], loc.at[2 + j])

    def row_out(j):
        lo, size = (TOP, LOW)[j]
        part_ = slice(lo, lo + size)
        return pltpu.make_async_copy(rg.at[:, part_], row_grad.at[:, part_], loc.at[4 + j])

    def pair_sum(j):
        heads.got(17 + j, lambda: pb.at[j])
        cg[j * 256 : j * 256 + 256, :] += pb[j].astype(F32)
        col_out(j).start()

    for h in range(2):
        for n in range(4):
            tasks["np%d%d" % (h, n)] = lambda h=h, n=n: near_put(h, n)
            tasks["na%d%d" % (h, n)] = lambda h=h, n=n: near_add(h, n)
        for j in range(2):
            tasks["z%s%d" % ("CD"[j], h)] = lambda h=h, j=j: z_second(h, j)
            tasks["zs%d%d" % (h, j)] = lambda h=h, j=j: z_sum(h, j)
    for j in range(2):
        tasks["pf%d" % j] = lambda j=j: pair_sum(j)


    def finish():
        rows.close()
        weights.close()
        near.close()
        heads.close(range(15))
        back.close((0, 1, 2, 3, 4, 5, 8, 9, 12, 13))
        rings.close((0, 1, 2, 3, 4, 5, 6, 7))
        back.got(3, lambda: yt.at[3])
        ring_wait("low0")
        ring_wait("top")

        def total(cols, *sources):
            lo, hi = cols[0], cols[0] + cols[1]

            def some(i, _):
                grad = r[at(own + i * 16, 16), lo:hi].astype(F32)
                for source in sources:
                    grad += source()[at(i * 16, 16), :].astype(F32)
                rg[at(i * 16, 16), lo:hi] = grad.astype(BF16)
                return 0

            lax.fori_loop(0, ROWS // 16, some, 0)

        total(TOP, lambda: tc.at[0], lambda: tc.at[1], lambda: yt.at[3])
        row_out(0).start()
        back.got(16, whole(yl))
        total(LOW, lambda: lc.at[0], lambda: lc.at[1], whole(yl))
        row_out(1).start()
        heads.got(15, whole(att_out))
        heads.got(16, whole(dq_out))

    tasks["fin"] = finish

    for step in STEPS:
        name, _, only = step.partition("@")

        def run(name=name):
            if name in tasks:
                tasks[name]()
            elif name[0] == "o":
                project(name[1:], "o")
            elif name[0] == "g":
                project(name[2:], name[1])
            elif name == "kt0":
                turn(0)
            elif name == "kt1":
                for each in given:
                    got_grads(each)
                turn(1)
            else:
                row_terms({"RA": "A", "RB": "B", "R1": "1", "R-1": "2", "R0": "3"}[name])

        if only:
            pl.when(me.core == int(only))(run)
        else:
            run()

    for wires in (rows, weights, heads, back, near, rings):
        wires.close()
    for j in range(2):
        col_out(j).wait()
        row_out(j).wait()


def results_kernel(enc, gain, row_grad, col_grad, att_in, dq_in, enc_grad, kg, vg, att, dq):
    wide = enc[...].astype(F32)
    factor = lax.rsqrt(jnp.mean(wide * wide, axis=-1, keepdims=True) + EPS)
    scaled = row_grad[...].astype(F32) * gain[...]
    inner = jnp.mean(scaled * wide, axis=-1, keepdims=True)
    enc_grad[...] = (factor * scaled - wide * (factor * factor * factor * inner)).astype(BF16)
    kg[...] = col_grad[0:HD, :].T
    vg[...] = col_grad[HD : 2 * HD, :].T
    att[...] = att_in[...]
    dq[...] = dq_in[...]


def on_device(enc_states, enc_gain, key_weight, value_weight, queries, out_grad, lengths):
    enc = enc_states[0]
    gain = enc_gain.reshape(1, D)
    vmem = pl.BlockSpec(memory_space=pltpu.VMEM)
    far = pl.BlockSpec(memory_space=pl.ANY)
    dma = pltpu.SemaphoreType.DMA
    shape = jax.ShapeDtypeStruct
    low = D - CUT

    row_grad, col_grad, att, dq = pl.pallas_call(
        kernel,
        out_shape=(
            shape((ROWS, D), BF16),
            shape((2 * HD, 512), F32),
            shape((TGT, HD), BF16),
            shape((TGT, HD), BF16),
        ),
        in_specs=[pl.BlockSpec(memory_space=pltpu.SMEM), vmem, vmem, far, far, far, far],
        out_specs=(far, far, far, far),
        scratch_shapes=[
            pltpu.VMEM((1024, D), BF16),
            pltpu.VMEM((D, 2 * HD), BF16),
            pltpu.VMEM((D, 2 * HD), BF16),
            pltpu.VMEM((2048, 2 * HD), BF16),
            pltpu.VMEM((1024, 2 * HD), BF16),
            pltpu.VMEM((TGT, HD), BF16),
            pltpu.VMEM((TGT, HD), BF16),
            pltpu.VMEM((TGT, 2048), BF16),
            pltpu.VMEM((TGT, 2048), BF16),
            pltpu.VMEM((TGT, HD), BF16),
            pltpu.VMEM((TGT, HD), BF16),
            pltpu.VMEM((2048, 2 * HD), BF16),
            pltpu.VMEM((1024, 2 * HD), BF16),
            pltpu.VMEM((2, 2 * HD, 1024), BF16),
            pltpu.VMEM((1024, D), BF16),
            pltpu.VMEM((4, ROWS, CUT), BF16),
            pltpu.VMEM((ROWS, CUT), BF16),
            pltpu.VMEM((2, ROWS, CUT), BF16),
            pltpu.VMEM((2, ROWS, low), BF16),
            pltpu.VMEM((4, ROWS, low), BF16),
            pltpu.VMEM((ROWS, low), BF16),
            pltpu.VMEM((8, 512, 512), BF16),
            pltpu.VMEM((2, 1536, 512), BF16),
            pltpu.VMEM((2, 256, 512), BF16),
            pltpu.VMEM((2, 256, 512), BF16),
            pltpu.VMEM((ROWS, D), BF16),
            pltpu.VMEM((2 * HD, 512), F32),
            dma((17,)),
            dma((17,)),
            dma((20,)),
            dma((20,)),
            dma((19,)),
            dma((19,)),
            dma((17,)),
            dma((17,)),
            dma((8,)),
            dma((8,)),
            dma((12,)),
            dma((12,)),
            dma((6,)),
            pltpu.SemaphoreType.REGULAR((2,)),
        ],
        compiler_params=pltpu.CompilerParams(
            collective_id=0, has_side_effects=True, vmem_limit_bytes=VMEM_BYTES
        ),
        name="gather_attend_scatter",
    )(lengths, enc, gain, key_weight, value_weight, queries[0], out_grad[0])

    def rows_of(count, width):
        return pl.BlockSpec((count, width), lambda i: (i, 0))

    enc_grad, kg, vg, att, dq = pl.pallas_call(
        results_kernel,
        grid=(2,),
        out_shape=(
            shape((ROWS, D), BF16),
            shape((512, HD), F32),
            shape((512, HD), F32),
            shape((TGT, HD), BF16),
            shape((TGT, HD), BF16),
        ),
        in_specs=[
            rows_of(64, D),
            pl.BlockSpec((1, D), lambda i: (0, 0)),
            rows_of(64, D),
            pl.BlockSpec((2 * HD, 256), lambda i: (0, i)),
            rows_of(256, HD),
            rows_of(256, HD),
        ],
        out_specs=(
            rows_of(64, D),
            rows_of(256, HD),
            rows_of(256, HD),
            rows_of(256, HD),
            rows_of(256, HD),
        ),
        name="results",
    )(enc, gain, row_grad, col_grad, att, dq)
    return (att[None], enc_grad[None], kg, vg, dq[None])


def solution(mesh):
    placed = (
        P(("section", "dp"), "seq", None),
        P(),
        P(None, "seq"),
        P(None, "seq"),
        P(("section", "dp"), None, "seq"),
        P(("section", "dp"), None, "seq"),
        P(),
    )
    return jax.shard_map(
        on_device,
        mesh=mesh,
        in_specs=placed,
        out_specs=(
            P(("section", "dp"), None, "seq"),
            P(("section", "dp"), "seq", None),
            P(("section", "dp"), "seq"),
            P(("section", "dp"), "seq"),
            P(("section", "dp"), None, "seq"),
        ),
        check_vma=False,
    )
```
